256 devices in a mesh: space: 16 (over y_hi, x, core), chan: 16 (over z, y_lo).
Axes of the slice: x: 4, y: 4 (y_hi: 2, y_lo: 2; y = y_hi * 2 + y_lo), z: 8, core: 2. Of those that a mesh axis runs over, the one named last changes fastest.
Arguments:
- inputs: bfloat16 [256, 48, 1024], P('chan', 'space'), may hold values from -6 to 6
- first_weight: bfloat16 [27, 256, 256], P(None, 'chan'), may hold values from -0.109375 to 0.109375
- second_weight: bfloat16 [27, 256, 256], P(None, 'chan'), may hold values from -0.109375 to 0.109375
- cotangent: bfloat16 [256, 48, 1024], P('chan', 'space'), may hold values from -6 to 6
Outputs:
- features: bfloat16 [256, 48, 1024], P('chan', 'space')
- grad_first: float32 [27, 256, 256], P(None, 'chan')
- grad_second: float32 [27, 256, 256], P(None, 'chan')
- grad_inputs: bfloat16 [256, 48, 1024], P('chan', 'space')
The draws below stay inside these ranges and needn't reach their ends.
All inputs are finite; a program needn't handle non-finite values.
Results may differ from the reference program's by a relative error of at most 0.025.
Values may be sent and summed in bfloat16 or wider, within the bound.
No kernel may reach another device: no remote copies, remote signals or barrier semaphores. Data moves between devices by JAX's collectives and lax.ppermute only.
A program may use at most 64 MiB of HBM per device.

```python
import jax
import jax.numpy as jnp
from jax import lax

C = 256
H = 32
TAPS = 27
DEPTH = 48
FLAT = 1024


def level_of(own_key, extent, split, low, high):
    gain = 1.0
    for dim, shards_of in split:
        steps = jax.random.uniform(jax.random.fold_in(jax.random.fold_in(own_key, 6), dim), (shards_of,), jnp.float32, low / len(split), high / len(split))
        gain = gain * jnp.repeat(jnp.exp(steps), extent[dim] // shards_of).reshape((-1,) + (1,) * (len(extent) - 1 - dim))
    return gain


def scatter_about(own_key, shape, scale, bound, pieces=(), held_as=jnp.bfloat16):
    values = scale * jax.random.normal(own_key, shape, jnp.float32)
    if pieces:
        values = values * level_of(own_key, shape, pieces, -0.22, 0.18)
    return jnp.clip(values, -bound, bound).astype(held_as)


def setup_inputs(seed: int = 0) -> dict:
    keys = jax.random.split(jax.random.key(seed), 5)
    return {
        "inputs": scatter_about(keys[0], (C, DEPTH, FLAT), 1.0, 6.0, ((0, 16), (1, 16))),
        "first_weight": scatter_about(keys[1], (TAPS, C, C), (TAPS * C // 2) ** -0.5, 0.109375, ((1, 16),)),
        "second_weight": scatter_about(keys[2], (TAPS, C, C), (TAPS * C // 2) ** -0.5, 0.109375, ((1, 16),)),
        "cotangent": scatter_about(keys[3], (C, DEPTH, FLAT), 1.0, 6.0, ((0, 16), (1, 16))),
    }


def offsets():
    return [(a, b, c) for a in (-1, 0, 1) for b in (-1, 0, 1) for c in (-1, 0, 1)]

def slope(value):
    sig = jax.nn.sigmoid(value)
    return sig * (1.0 + value * (1.0 - sig))

def move(source, depth_step, row_step, col_step, base, depth, width):
    flat = source.shape[2]
    slab = lax.slice_in_dim(source, base + depth_step, base + depth_step + depth, axis=1)
    margin = width + 1
    wide = jnp.pad(slab, ((0, 0), (0, 0), (margin, margin)))
    begin = margin + row_step * width + col_step
    moved = lax.slice_in_dim(wide, begin, begin + flat, axis=2)
    column = jnp.arange(flat, dtype=jnp.int32) % width + col_step
    keep = (column >= 0) & (column < width)
    return jnp.where(keep, moved, jnp.zeros_like(moved))

def forward_conv(field, weight):
    depth = field.shape[1]
    padded = jnp.pad(field.astype(jnp.float32), ((0, 0), (1, 1), (0, 0)))
    total = jnp.zeros((weight.shape[1], depth, field.shape[2]), jnp.float32)
    for k, (a, b, c) in enumerate(offsets()):
        shifted = move(padded, a, b, c, 1, depth, H)
        total = total + jnp.einsum('oi,idp->odp', weight[k].astype(jnp.float32), shifted)
    return total

def data_grad(err, weight):
    depth = err.shape[1]
    padded = jnp.pad(err.astype(jnp.float32), ((0, 0), (1, 1), (0, 0)))
    total = jnp.zeros((weight.shape[2], depth, err.shape[2]), jnp.float32)
    for k, (a, b, c) in enumerate(offsets()):
        shifted = move(padded, -a, -b, -c, 1, depth, H)
        total = total + jnp.einsum('oi,odp->idp', weight[k].astype(jnp.float32), shifted)
    return total

def weight_grad(field, err):
    depth = field.shape[1]
    padded = jnp.pad(field.astype(jnp.float32), ((0, 0), (1, 1), (0, 0)))
    spread = jnp.pad(err.astype(jnp.float32), ((0, 0), (2, 2), (0, 0)))
    terms = []
    for k, (a, b, c) in enumerate(offsets()):
        shifted = move(spread, -a, -b, -c, 1, depth + 2, H)
        terms.append(jnp.einsum('idp,odp->oi', padded, shifted))
    return jnp.stack(terms)

def reference(inputs, first_weight, second_weight, cotangent):
    pre_first = forward_conv(inputs, first_weight)
    hidden = jax.nn.silu(pre_first).astype(jnp.bfloat16)
    pre_second = forward_conv(hidden, second_weight)
    features = jax.nn.silu(pre_second).astype(jnp.bfloat16)
    err_second = (cotangent.astype(jnp.float32) * slope(pre_second)).astype(jnp.bfloat16)
    grad_second = weight_grad(hidden, err_second)
    grad_hidden = data_grad(err_second, second_weight).astype(jnp.bfloat16)
    err_first = (grad_hidden.astype(jnp.float32) * slope(pre_first)).astype(jnp.bfloat16)
    grad_first = weight_grad(inputs, err_first)
    grad_inputs = data_grad(err_first, first_weight).astype(jnp.bfloat16)
    return (features, grad_first, grad_second, grad_inputs)
```

```python
import functools

import jax
import jax.numpy as jnp
import numpy as np
from jax import lax
from jax.experimental import pallas as pl
from jax.experimental.pallas import tpu as pltpu
from jax.sharding import PartitionSpec as P

SIDE = 32
FLAT = SIDE * SIDE
PLANES = 3
PIECE = 16
SLOTS = 4
BLOCK = SLOTS * PIECE
TAPS = 27
ROWS = 9 * BLOCK
COLS = 3 * BLOCK
NEAR = (0, 1, 2, 3)
FAR = (0, 4, 8, 12)
LIMIT = 24 * 1024 * 1024
BF = jnp.bfloat16
F32 = jnp.float32


def call(body, outs, scratch, scalars, arrays, flops):
    moved = sum(int(np.prod(x.shape)) * x.dtype.itemsize for x in (*arrays, *outs))
    spec = pl.BlockSpec(memory_space=pltpu.VMEM)
    return pl.pallas_call(
        body,
        out_shape=outs,
        in_specs=[pl.BlockSpec(memory_space=pltpu.SMEM)] * len(scalars) + [spec] * len(arrays),
        out_specs=[spec] * len(outs),
        scratch_shapes=scratch,
        compiler_params=pltpu.CompilerParams(vmem_limit_bytes=LIMIT),
        cost_estimate=pl.CostEstimate(flops=flops, bytes_accessed=moved, transcendentals=0),
    )(*scalars, *arrays)


def shape(dims, dtype=BF):
    return jax.ShapeDtypeStruct(dims, dtype)


def chosen(chan, take, give):
    row = lax.broadcasted_iota(jnp.int32, (256, 256), 0)
    col = lax.broadcasted_iota(jnp.int32, (256, 256), 1)
    n, m = col // BLOCK, (col // PIECE) % SLOTS
    block = chan ^ (n * give[1]) ^ (m * take[1])
    return (row == block * PIECE + col % PIECE).astype(BF)


def split_body(take, give, chan_ref, weight_ref, *out_refs):
    pick = chosen(chan_ref[0], take, give)
    moved = jnp.dot(weight_ref[...], pick, preferred_element_type=F32).astype(BF)
    for n in range(SLOTS):
        out_refs[n][...] = moved[:, n * BLOCK : (n + 1) * BLOCK]


def split_weight(chan, weight, take, give):
    rows = TAPS * PIECE
    return call(
        functools.partial(split_body, take, give),
        [shape((rows, BLOCK))] * SLOTS,
        [],
        [chan],
        [weight.reshape(rows, 256)],
        2 * rows * 256 * 256,
    )


def arrange_body(*refs):
    pieces, (fwd_ref, bwd_ref) = refs[:SLOTS], refs[SLOTS:]
    for a in range(3):
        for q in range(9):
            k = 9 * a + q
            block = jnp.concatenate([p[PIECE * k : PIECE * (k + 1), :] for p in pieces], axis=0)
            fwd_ref[BLOCK * q : BLOCK * (q + 1), BLOCK * a : BLOCK * (a + 1)] = block
            turned = block.astype(F32).T.astype(BF)
            bwd_ref[BLOCK * (8 - q) : BLOCK * (9 - q), BLOCK * (2 - a) : BLOCK * (3 - a)] = turned


def arrange_weight(pieces):
    return call(arrange_body, [shape((ROWS, COLS))] * 2, [], [], pieces, 0)


def edges():
    cell = lax.broadcasted_iota(jnp.int32, (1, FLAT), 1)
    col = cell % SIDE
    return cell, col


def fill(odd, slots, off_ref, core_ref, field):
    for p in range(PLANES):
        for m in range(SLOTS):
            field[BLOCK * (p + 1) + PIECE * m : BLOCK * (p + 1) + PIECE * (m + 1), :] = slots[m][p]
    off, core = off_ref[...].reshape(BLOCK, FLAT), core_ref[...].reshape(BLOCK, FLAT)
    field[:BLOCK, :] = jnp.where(odd, core, off)
    field[BLOCK * (PLANES + 1) :, :] = jnp.where(odd, off, core)


def conv_body(space_ref, weight_ref, s0, s1, s2, s3, off_ref, core_ref, own_ref, o1, o2, o3, field):
    fill(space_ref[0] % 2 == 1, (s0, s1, s2, s3), off_ref, core_ref, field)
    cell, col = edges()
    weight = weight_ref[...]
    for d in range(PLANES):
        terms = jnp.dot(weight, field[BLOCK * d : BLOCK * d + COLS, :], preferred_element_type=F32)
        sums = []
        for c in range(3):
            up, mid, down = (terms[BLOCK * (3 * b + c) : BLOCK * (3 * b + c + 1)] for b in range(3))
            down = jnp.where(cell < FLAT - SIDE, pltpu.roll(down, FLAT - SIDE, 1), 0.0)
            up = jnp.where(cell >= SIDE, pltpu.roll(up, SIDE, 1), 0.0)
            sums.append(mid + down + up)
        left = jnp.where(col >= 1, pltpu.roll(sums[0], 1, 1), 0.0)
        right = jnp.where(col < SIDE - 1, pltpu.roll(sums[2], FLAT - 1, 1), 0.0)
        total = sums[1] + left + right
        own_ref[d] = total[:PIECE]
        for n, out in enumerate((o1, o2, o3), 1):
            out[d] = total[PIECE * n : PIECE * (n + 1)].astype(BF)


def conv(space, weight, slots, off, core):
    piece = (PLANES, PIECE, FLAT)
    return call(
        conv_body,
        [shape(piece, F32)] + [shape(piece)] * 3,
        [pltpu.VMEM((BLOCK * (PLANES + 2), FLAT), BF)],
        [space],
        [weight, *slots, off, core],
        2 * ROWS * COLS * FLAT * PLANES,
    )


def grad_body(space_ref, s0, s1, s2, s3, off_ref, core_ref, e0, e1, e2, e3, *rest):
    outs, (field, moved) = rest[:SLOTS], rest[SLOTS:]
    fill(space_ref[0] % 2 == 1, (s0, s1, s2, s3), off_ref, core_ref, field)
    cell, col = edges()
    total = jnp.zeros((ROWS, COLS), F32)
    for d in range(PLANES):
        err = jnp.concatenate([e[d] for e in (e0, e1, e2, e3)], axis=0).astype(F32)
        for c in range(3):
            if c == 0:
                one = jnp.where(col < SIDE - 1, pltpu.roll(err, FLAT - 1, 1), 0.0)
            elif c == 2:
                one = jnp.where(col >= 1, pltpu.roll(err, 1, 1), 0.0)
            else:
                one = err
            for b in range(3):
                if b == 0:
                    two = jnp.where(cell < FLAT - SIDE, pltpu.roll(one, FLAT - SIDE, 1), 0.0)
                elif b == 2:
                    two = jnp.where(cell >= SIDE, pltpu.roll(one, SIDE, 1), 0.0)
                else:
                    two = one
                two = two.astype(BF)
                for n in range(SLOTS):
                    at = n * 9 * PIECE + (3 * b + c) * PIECE
                    moved[at : at + PIECE, :] = two[PIECE * n : PIECE * (n + 1)]
        total = total + lax.dot_general(
            moved[...],
            field[BLOCK * d : BLOCK * d + COLS, :],
            (((1,), (1,)), ((), ())),
            preferred_element_type=F32,
        )
    for n in range(SLOTS):
        outs[n][...] = total[n * 9 * PIECE : (n + 1) * 9 * PIECE].astype(BF)


def weight_grad(space, slots, off, core, errs):
    return call(
        grad_body,
        [shape((9 * PIECE, COLS))] * SLOTS,
        [pltpu.VMEM((BLOCK * (PLANES + 2), FLAT), BF), pltpu.VMEM((ROWS, FLAT), BF)],
        [space],
        [*slots, off, core, *errs],
        2 * ROWS * COLS * FLAT * PLANES,
    )


def finish_body(chan_ref, sum_ref, first_ref, second_ref):
    for layer, (out, take, give) in enumerate(((first_ref, NEAR, FAR), (second_ref, FAR, NEAR))):
        pick = chosen(chan_ref[0], take, give)
        for a in range(3):
            parts = [
                sum_ref[layer * SLOTS + n, :, a * BLOCK : (a + 1) * BLOCK] for n in range(SLOTS)
            ]
            wide = jnp.concatenate(parts, axis=1)
            back = lax.dot_general(wide, pick, (((1,), (1,)), ((), ())), preferred_element_type=F32)
            out[9 * a : 9 * (a + 1)] = back.reshape(9, PIECE, 256)


def finish(chan, total):
    return call(
        finish_body,
        [shape((TAPS, PIECE, 256), F32)] * 2,
        [],
        [chan],
        [total],
        2 * 2 * TAPS * PIECE * 256 * 256,
    )


def swap(piece, mask):
    return lax.ppermute(piece, "chan", [(i, i ^ mask) for i in range(16)])


def gather(piece, masks):
    return [piece] + [swap(piece, mask) for mask in masks[1:]]


def halo(space, slots):
    odd = space[0] % 2 == 1
    first = jnp.stack([s[0] for s in slots])
    last = jnp.stack([s[PLANES - 1] for s in slots])
    outward = [(i, i + 1 if i % 2 else i - 1) for i in range(1, 15)]
    inward = [(i, i ^ 1) for i in range(16)]
    off = lax.ppermute(jnp.where(odd, last, first), "space", outward)
    core = lax.ppermute(jnp.where(odd, first, last), "space", inward)
    return off, core


def scatter(pieces, masks):
    own, rest = pieces[0], pieces[1:]
    got = [swap(p, mask) for p, mask in zip(rest, masks[1:])]
    return own.astype(F32) + got[0].astype(F32) + got[1].astype(F32) + got[2].astype(F32)


def total_over_space(grads):
    width = grads.shape[-1]
    parts = grads.reshape(16, -1, width)
    got = lax.all_to_all(parts, "space", 0, 0, tiled=True)
    mine = got.astype(F32).sum(axis=0).astype(BF)
    spread = jnp.broadcast_to(mine[None], parts.shape)
    return lax.all_to_all(spread, "space", 0, 0, tiled=True).reshape(grads.shape)


def slope(value):
    sig = jax.nn.sigmoid(value)
    return sig * (1.0 + value * (1.0 - sig))


def shards(inputs, first_weight, second_weight, cotangent):
    space = lax.axis_index("space").astype(jnp.int32).reshape(1)
    chan = lax.axis_index("chan").astype(jnp.int32).reshape(1)
    inputs = inputs.transpose(1, 0, 2)
    cotangent = cotangent.transpose(1, 0, 2)

    def weights(weight, take, give):
        parts = split_weight(chan, weight, take, give)
        return arrange_weight([parts[0]] + [swap(p, m) for p, m in zip(parts[1:], give[1:])])

    in_slots = gather(inputs, NEAR)
    in_edge = halo(space, in_slots)
    fwd_first, bwd_first = weights(first_weight, NEAR, FAR)
    pre_first = scatter(conv(space, fwd_first, in_slots, *in_edge), FAR)
    hidden = jax.nn.silu(pre_first).astype(BF)

    fwd_second, bwd_second = weights(second_weight, FAR, NEAR)
    hid_slots = gather(hidden, FAR)
    hid_edge = halo(space, hid_slots)
    pre_second = scatter(conv(space, fwd_second, hid_slots, *hid_edge), NEAR)
    features = jax.nn.silu(pre_second).astype(BF)
    err_second = (cotangent.astype(F32) * slope(pre_second)).astype(BF)

    err2_slots = gather(err_second, NEAR)
    err2_edge = halo(space, err2_slots)
    grad_hidden = scatter(conv(space, bwd_second, err2_slots, *err2_edge), FAR).astype(BF)
    err_first = (grad_hidden.astype(F32) * slope(pre_first)).astype(BF)
    grads_second = weight_grad(space, hid_slots, *hid_edge, err2_slots)

    err1_slots = gather(err_first, FAR)
    grads_first = weight_grad(space, in_slots, *in_edge, err1_slots)
    err1_edge = halo(space, err1_slots)
    grad_inputs = scatter(conv(space, bwd_first, err1_slots, *err1_edge), NEAR).astype(BF)

    grads = [grads_first[0]] + [swap(p, m) for p, m in zip(grads_first[1:], FAR[1:])]
    grads += [grads_second[0]] + [swap(p, m) for p, m in zip(grads_second[1:], NEAR[1:])]
    grad_first, grad_second = finish(chan, total_over_space(jnp.stack(grads)))
    return (
        features.transpose(1, 0, 2),
        grad_first,
        grad_second,
        grad_inputs.transpose(1, 0, 2),
    )


def solution(mesh):
    slab = P("chan", "space", None)
    filters = P(None, "chan", None)
    return jax.shard_map(
        shards,
        mesh=mesh,
        in_specs=(slab, filters, filters, slab),
        out_specs=(slab, filters, filters, slab),
        check_vma=False,
    )
```

```python
import functools

import jax
import jax.numpy as jnp
import numpy as np
from jax import lax
from jax.experimental import pallas as pl
from jax.experimental.pallas import tpu as pltpu
from jax.sharding import PartitionSpec as P

SIDE = 32
FLAT = SIDE * SIDE
PLANES = 3
PIECE = 16
SLOTS = 4
BLOCK = SLOTS * PIECE
TAPS = 27
ROWS = 9 * BLOCK
COLS = 3 * BLOCK
NEAR = (0, 1, 2, 3)
FAR = (0, 4, 8, 12)
FIRST, SECOND = (FAR, NEAR), (NEAR, FAR)
LIMIT = 24 * 1024 * 1024
BF = jnp.bfloat16
F32 = jnp.float32


def call(body, outs, scratch, scalars, arrays, flops):
    moved = sum(int(np.prod(x.shape)) * x.dtype.itemsize for x in (*arrays, *outs))
    spec = pl.BlockSpec(memory_space=pltpu.VMEM)
    return pl.pallas_call(
        body,
        out_shape=outs,
        in_specs=[pl.BlockSpec(memory_space=pltpu.SMEM)] * len(scalars) + [spec] * len(arrays),
        out_specs=[spec] * len(outs),
        scratch_shapes=scratch,
        compiler_params=pltpu.CompilerParams(vmem_limit_bytes=LIMIT),
        cost_estimate=pl.CostEstimate(flops=flops, bytes_accessed=moved, transcendentals=0),
    )(*scalars, *arrays)


def shape(dims, dtype=BF):
    return jax.ShapeDtypeStruct(dims, dtype)


def chosen(chan, take, give):
    row = lax.broadcasted_iota(jnp.int32, (256, 256), 0)
    col = lax.broadcasted_iota(jnp.int32, (256, 256), 1)
    n, m = col // BLOCK, (col // PIECE) % SLOTS
    block = chan ^ (n * give[1]) ^ (m * take[1])
    return (row == block * PIECE + col % PIECE).astype(BF)


HALF = 14 * PIECE
TALL, SPLIT = 9 * PIECE, 5 * PIECE
GRAD_ROWS = TALL + SPLIT
HELD = SLOTS * GRAD_ROWS
LANES = 2 * BLOCK


def split_body(take, give, chan_ref, weight_ref, *out_refs):
    pick = chosen(chan_ref[0], take, give)
    moved = jnp.dot(weight_ref[...], pick, preferred_element_type=F32).astype(BF)
    for n, out in enumerate(out_refs):
        part = moved[:, n * BLOCK : (n + 1) * BLOCK]
        out[:, :BLOCK] = part[:HALF]
        out[: HALF - PIECE, BLOCK:] = part[HALF:]
        out[HALF - PIECE :, BLOCK:] = jnp.zeros((PIECE, BLOCK), BF)


def split_weight(chan, weight, take, give):
    rows = TAPS * PIECE
    return call(
        functools.partial(split_body, take, give),
        [shape((HALF, 2 * BLOCK))] * SLOTS,
        [],
        [chan],
        [weight.reshape(rows, 256)],
        2 * rows * 256 * 256,
    )


def arrange_body(*refs):
    pieces, (fwd_ref, bwd_ref) = refs[:SLOTS], refs[SLOTS:]
    for a in range(3):
        for q in range(9):
            k = 9 * a + q
            row, lane = PIECE * (k % 14), BLOCK * (k // 14)
            block = jnp.concatenate([p[row : row + PIECE, lane : lane + BLOCK] for p in pieces], axis=0)
            fwd_ref[BLOCK * q : BLOCK * (q + 1), BLOCK * a : BLOCK * (a + 1)] = block
            turned = block.astype(F32).T.astype(BF)
            bwd_ref[BLOCK * (8 - q) : BLOCK * (9 - q), BLOCK * (2 - a) : BLOCK * (3 - a)] = turned


def arrange_weight(pieces):
    return call(arrange_body, [shape((ROWS, COLS))] * 2, [], [], pieces, 0)


def edges():
    cell = lax.broadcasted_iota(jnp.int32, (1, FLAT), 1)
    col = cell % SIDE
    return cell, col


def fill(odd, slots, edge, field):
    if edge:
        for p in range(PLANES):
            for m in range(SLOTS):
                at = BLOCK * (p + 1) + PIECE * m
                field[at : at + PIECE, :] = slots[m][p]
        off, core = (ref[...].reshape(BLOCK, FLAT) for ref in edge)
        field[:BLOCK, :] = jnp.where(odd, core, off)
        field[BLOCK * (PLANES + 1) :, :] = jnp.where(odd, off, core)
    else:
        for p in range(PLANES + 2):
            for m in range(SLOTS):
                at = BLOCK * p + PIECE * m
                field[at : at + PIECE, :] = slots[m][p]


def conv_body(space_ref, weight_ref, *refs):
    slots, edge = refs[:SLOTS], refs[SLOTS:-5]
    own_ref, o1, o2, o3, field = refs[-5:]
    fill(space_ref[0] % 2 == 1, slots, edge, field)
    cell, col = edges()
    weight = weight_ref[...]
    for d in range(PLANES):
        terms = jnp.dot(weight, field[BLOCK * d : BLOCK * d + COLS, :], preferred_element_type=F32)
        sums = []
        for c in range(3):
            up, mid, down = (terms[BLOCK * (3 * b + c) : BLOCK * (3 * b + c + 1)] for b in range(3))
            down = jnp.where(cell < FLAT - SIDE, pltpu.roll(down, FLAT - SIDE, 1), 0.0)
            up = jnp.where(cell >= SIDE, pltpu.roll(up, SIDE, 1), 0.0)
            sums.append(mid + down + up)
        left = jnp.where(col >= 1, pltpu.roll(sums[0], 1, 1), 0.0)
        right = jnp.where(col < SIDE - 1, pltpu.roll(sums[2], FLAT - 1, 1), 0.0)
        total = sums[1] + left + right
        own_ref[d] = total[:PIECE].astype(own_ref.dtype)
        for n, out in enumerate((o1, o2, o3), 1):
            out[d] = total[PIECE * n : PIECE * (n + 1)].astype(BF)


def conv(space, weight, slots, edge=(), own=F32):
    piece = (PLANES, PIECE, FLAT)
    return call(
        conv_body,
        [shape(piece, own)] + [shape(piece)] * 3,
        [pltpu.VMEM((BLOCK * (PLANES + 2), FLAT), BF)],
        [space],
        [weight, *slots, *edge],
        2 * ROWS * COLS * FLAT * PLANES,
    )


def moves(err, cell, col):
    for c in range(3):
        if c == 0:
            one = jnp.where(col < SIDE - 1, pltpu.roll(err, FLAT - 1, 1), 0.0)
        elif c == 2:
            one = jnp.where(col >= 1, pltpu.roll(err, 1, 1), 0.0)
        else:
            one = err
        for b in range(3):
            if b == 0:
                two = jnp.where(cell < FLAT - SIDE, pltpu.roll(one, FLAT - SIDE, 1), 0.0)
            elif b == 2:
                two = jnp.where(cell >= SIDE, pltpu.roll(one, SIDE, 1), 0.0)
            else:
                two = one
            yield 3 * b + c, two.astype(BF)


def across(lhs, rhs):
    return lax.dot_general(lhs, rhs, (((1,), (1,)), ((), ())), preferred_element_type=F32)


def grad_body(space_ref, s0, s1, s2, s3, off_ref, core_ref, e0, e1, e2, e3, *rest):
    outs, (field, moved) = rest[:SLOTS], rest[SLOTS:]
    fill(space_ref[0] % 2 == 1, (s0, s1, s2, s3), (off_ref, core_ref), field)
    cell, col = edges()
    total = jnp.zeros((ROWS, COLS), F32)
    for d in range(PLANES):
        err = jnp.concatenate([e[d] for e in (e0, e1, e2, e3)], axis=0).astype(F32)
        for q, two in moves(err, cell, col):
            for n in range(SLOTS):
                at = n * TALL + q * PIECE
                moved[at : at + PIECE, :] = two[PIECE * n : PIECE * (n + 1)]
        total = total + across(moved[...], field[BLOCK * d : BLOCK * d + COLS, :])
    for n in range(SLOTS):
        part = total[n * TALL : (n + 1) * TALL].astype(BF)
        outs[n][:TALL, :] = part[:, : 2 * BLOCK]
        outs[n][TALL:, :BLOCK] = part[:SPLIT, 2 * BLOCK :]
        outs[n][TALL : GRAD_ROWS - PIECE, BLOCK:] = part[SPLIT:, 2 * BLOCK :]
        outs[n][GRAD_ROWS - PIECE :, BLOCK:] = jnp.zeros((PIECE, BLOCK), BF)


def weight_grad(space, slots, edge, errs):
    return call(
        grad_body,
        [shape((GRAD_ROWS, LANES))] * SLOTS,
        [pltpu.VMEM((BLOCK * (PLANES + 2), FLAT), BF), pltpu.VMEM((ROWS, FLAT), BF)],
        [space],
        [*slots, *edge, *errs],
        2 * ROWS * COLS * FLAT * PLANES,
    )


def keep_body(space_ref, *refs):
    odd = space_ref[0] % 2 == 1
    pieces, (keep_ref, give_ref) = refs[:-2], refs[-2:]
    for n in range(SLOTS):
        first, second = pieces[n][...], pieces[SLOTS + n][...]
        rows = slice(n * GRAD_ROWS, (n + 1) * GRAD_ROWS)
        keep_ref[rows, :] = jnp.where(odd, second, first)
        give_ref[rows, :] = jnp.where(odd, first, second)


def fold_body(shift, count, space_ref, *refs):
    got, outs, held = refs[: -count - 1], refs[-count - 1 : -1], refs[-1]
    total = got[0][...].astype(F32)
    for ref in got[1:]:
        total = total + ref[...].astype(F32)
    held[...] = total
    part = outs[0].shape[0]
    at = (space_ref[0] >> shift) % count
    for m, out in enumerate(outs):
        out[...] = held[pl.ds(pl.multiple_of((at ^ m) * part, PIECE), part), :].astype(BF)


def fold(space, pieces, shift, count):
    rows = pieces[0].shape[0]
    return call(
        functools.partial(fold_body, shift, count),
        [shape((rows // count, LANES))] * count,
        [pltpu.VMEM((rows, LANES), F32)],
        [space],
        pieces,
        0,
    )


def join_body(shift, space_ref, *refs):
    out, count = refs[-1], len(refs) - 1
    part = refs[0].shape[0]
    at = (space_ref[0] >> shift) % count
    for m, ref in enumerate(refs[:-1]):
        out[pl.ds(pl.multiple_of((at ^ m) * part, PIECE), part), :] = ref[...]


def join(space, pieces, shift):
    rows = pieces[0].shape[0] * len(pieces)
    return call(
        functools.partial(join_body, shift), [shape((rows, LANES))], [], [space], pieces, 0
    )[0]


def finish_body(space_ref, chan_ref, mine_ref, got_ref, first_ref, second_ref):
    odd = space_ref[0] % 2 == 1
    first = jnp.where(odd, got_ref[...], mine_ref[...])
    second = jnp.where(odd, mine_ref[...], got_ref[...])
    for held, out, (take, give) in ((first, first_ref, FIRST), (second, second_ref, SECOND)):
        pick = chosen(chan_ref[0], take, give)
        for a in range(3):
            parts = []
            for n in range(SLOTS):
                at = n * GRAD_ROWS
                if a < 2:
                    parts.append(held[at : at + TALL, a * BLOCK : (a + 1) * BLOCK])
                else:
                    high = held[at + TALL : at + GRAD_ROWS, :BLOCK]
                    low = held[at + TALL : at + GRAD_ROWS - PIECE, BLOCK:]
                    parts.append(jnp.concatenate([high, low], axis=0))
            wide = jnp.concatenate(parts, axis=1)
            out[9 * a : 9 * (a + 1)] = across(wide, pick).reshape(9, PIECE, 256)


def finish(space, chan, mine, got):
    return call(
        finish_body,
        [shape((TAPS, PIECE, 256), F32)] * 2,
        [],
        [space, chan],
        [mine, got],
        2 * TAPS * PIECE * 256 * 256,
    )


def by_chan(array, mask):
    return lax.ppermute(array, "chan", [(i, i ^ mask) for i in range(16)]) if mask else array


def by_space(array, mask):
    return lax.ppermute(array, "space", [(i, i ^ mask) for i in range(16)])


def over_chan(arrays, masks):
    return [by_chan(array, mask) for array, mask in zip(arrays, masks)]


def gather(array, masks):
    return over_chan([array] * SLOTS, masks)


def halo(odd, first, last):
    outward = [(i, i + 1 if i % 2 else i - 1) for i in range(1, 15)]
    off = lax.ppermute(jnp.where(odd, last, first), "space", outward)
    return off, by_space(jnp.where(odd, first, last), 1)


def slot_halo(odd, slots):
    first = jnp.stack([s[0] for s in slots])
    last = jnp.stack([s[PLANES - 1] for s in slots])
    return halo(odd, first, last)


def add(pieces):
    total = pieces[0].astype(F32)
    for piece in pieces[1:]:
        total = total + piece.astype(F32)
    return total


def slope(value):
    sig = jax.nn.sigmoid(value)
    return sig * (1.0 + value * (1.0 - sig))


def total_over_space(space, chan, first, second):
    keep, give = call(
        keep_body, [shape((HELD, LANES))] * 2, [], [space], [*first, *second], 0
    )
    mine, *rest = fold(space, [keep, by_space(give, 1)], 1, 4)
    mine = fold(space, [mine] + [by_space(r, 2 * m) for m, r in enumerate(rest, 1)], 0, 1)[0]
    mine = fold(space, [mine, by_space(mine, 8)], 0, 1)[0]
    mine = join(space, [mine] + [by_space(mine, 2 * m) for m in (1, 2, 3)], 1)
    return finish(space, chan, mine, by_space(mine, 1))


tie = lax.optimization_barrier


def shards(inputs, first_weight, second_weight, cotangent):
    space = lax.axis_index("space").astype(jnp.int32).reshape(1)
    chan = lax.axis_index("chan").astype(jnp.int32).reshape(1)
    odd = space[0] % 2 == 1
    inputs = inputs.transpose(1, 0, 2)
    cotangent = cotangent.transpose(1, 0, 2)

    in_slots = gather(inputs, FAR)
    pieces = over_chan(split_weight(chan, first_weight, *FIRST), NEAR)
    in_slots, pieces = tie((in_slots, pieces))
    in_edge = slot_halo(odd, in_slots)
    fwd_first, bwd_first = arrange_weight(pieces)
    pieces = over_chan(split_weight(chan, second_weight, *SECOND), FAR)
    in_edge, pieces = tie((in_edge, pieces))
    pre_first = add(over_chan(conv(space, fwd_first, in_slots, in_edge), NEAR))
    hidden = jax.nn.silu(pre_first).astype(BF)

    hid_slots = gather(hidden, NEAR)
    fwd_second, bwd_second = arrange_weight(pieces)
    hid_edge = slot_halo(odd, hid_slots)
    pre_second = add(over_chan(conv(space, fwd_second, hid_slots, hid_edge), FAR))
    features = jax.nn.silu(pre_second).astype(BF)
    err_second = (cotangent.astype(F32) * slope(pre_second)).astype(BF)

    err2_slots = gather(err_second, FAR)
    err2_edge = slot_halo(odd, err2_slots)
    grads = weight_grad(space, hid_slots, hid_edge, err2_slots)
    err2_edge, grads = tie((err2_edge, grads))
    sums = over_chan(conv(space, bwd_second, err2_slots, err2_edge), NEAR)
    back_second = over_chan(grads, FAR)
    sums, back_second = tie((sums, back_second))
    grad_hidden = add(sums).astype(BF)
    err_first = (grad_hidden.astype(F32) * slope(pre_first)).astype(BF)

    err1_slots = gather(err_first, NEAR)
    grads = weight_grad(space, in_slots, in_edge, err1_slots)
    err1_slots, grads = tie((err1_slots, grads))
    back_first = over_chan(grads, NEAR)
    grad_first, grad_second = total_over_space(space, chan, back_first, back_second)
    err1_edge = slot_halo(odd, err1_slots)
    sums = over_chan(conv(space, bwd_first, err1_slots, err1_edge), FAR)
    grad_inputs = add(sums).astype(BF)
    return (
        features.transpose(1, 0, 2),
        grad_first,
        grad_second,
        grad_inputs.transpose(1, 0, 2),
    )


def solution(mesh):
    slab = P("chan", "space", None)
    filters = P(None, "chan", None)
    return jax.shard_map(
        shards,
        mesh=mesh,
        in_specs=(slab, filters, filters, slab),
        out_specs=(slab, filters, filters, slab),
        check_vma=False,
    )
```

```python
import functools

import jax
import jax.numpy as jnp
import numpy as np
from jax import lax
from jax.experimental import pallas as pl
from jax.experimental.pallas import tpu as pltpu
from jax.sharding import PartitionSpec as P

SIDE = 32
FLAT = SIDE * SIDE
PLANES = 3
PIECE = 16
SLOTS = 4
BLOCK = SLOTS * PIECE
TAPS = 27
ROWS = 9 * BLOCK
COLS = 3 * BLOCK
NEAR = (0, 1, 2, 3)
FAR = (0, 4, 8, 12)
FIRST, SECOND = (FAR, NEAR), (NEAR, FAR)
LIMIT = 24 * 1024 * 1024
BF = jnp.bfloat16
F32 = jnp.float32


def call(body, outs, scratch, scalars, arrays, flops):
    moved = sum(int(np.prod(x.shape)) * x.dtype.itemsize for x in (*arrays, *outs))
    spec = pl.BlockSpec(memory_space=pltpu.VMEM)
    return pl.pallas_call(
        body,
        out_shape=outs,
        in_specs=[pl.BlockSpec(memory_space=pltpu.SMEM)] * len(scalars) + [spec] * len(arrays),
        out_specs=[spec] * len(outs),
        scratch_shapes=scratch,
        compiler_params=pltpu.CompilerParams(vmem_limit_bytes=LIMIT),
        cost_estimate=pl.CostEstimate(flops=flops, bytes_accessed=moved, transcendentals=0),
    )(*scalars, *arrays)


def shape(dims, dtype=BF):
    return jax.ShapeDtypeStruct(dims, dtype)


def chosen(chan, take, give):
    row = lax.broadcasted_iota(jnp.int32, (256, 256), 0)
    col = lax.broadcasted_iota(jnp.int32, (256, 256), 1)
    n, m = col // BLOCK, (col // PIECE) % SLOTS
    block = chan ^ (n * give[1]) ^ (m * take[1])
    return (row == block * PIECE + col % PIECE).astype(BF)


HALF = 14 * PIECE
TALL, SPLIT = 9 * PIECE, 5 * PIECE
GRAD_ROWS = TALL + SPLIT
HELD = SLOTS * GRAD_ROWS
PLAIN = ((0, 0), (1, 0), (2, 0), (3, 0))
PASSED = ((0, 0), (1, 0), (1, HALF), (2, 0))
ARRIVED = ((0, 0), (1, 0), (2, HALF), (2, 0))
LANES = 2 * BLOCK


def split_body(take, give, spots, chan_ref, weight_ref, *out_refs):
    pick = chosen(chan_ref[0], take, give)
    moved = jnp.dot(weight_ref[...], pick, preferred_element_type=F32).astype(BF)
    for n, (k, row) in enumerate(spots):
        part, out = moved[:, n * BLOCK : (n + 1) * BLOCK], out_refs[k]
        out[row : row + HALF, :BLOCK] = part[:HALF]
        out[row : row + HALF - PIECE, BLOCK:] = part[HALF:]
        out[row + HALF - PIECE : row + HALF, BLOCK:] = jnp.zeros((PIECE, BLOCK), BF)


def split_weight(chan, weight, take, give, sent):
    rows = TAPS * PIECE
    return call(
        functools.partial(split_body, take, give, sent),
        [shape((HALF * sum(k == j for k, _ in sent), LANES)) for j in range(1 + max(sent)[0])],
        [],
        [chan],
        [weight.reshape(rows, 256)],
        2 * rows * 256 * 256,
    )


def stitch_body(left_ref, right_ref, out_ref):
    out_ref[:HALF, :] = left_ref[...]
    out_ref[HALF:, :] = right_ref[HALF:, :]


def stitch(left, right):
    return call(stitch_body, [shape((2 * HALF, LANES))], [], [], [left, right], 0)[0]


def arrange_body(spots, *refs):
    fwd_ref, bwd_ref = refs[-2:]
    for a in range(3):
        for q in range(9):
            k = 9 * a + q
            row, lane = PIECE * (k % 14), BLOCK * (k // 14)
            block = jnp.concatenate(
                [refs[j][at + row : at + row + PIECE, lane : lane + BLOCK] for j, at in spots], axis=0
            )
            fwd_ref[BLOCK * q : BLOCK * (q + 1), BLOCK * a : BLOCK * (a + 1)] = block
            turned = block.astype(F32).T.astype(BF)
            bwd_ref[BLOCK * (8 - q) : BLOCK * (9 - q), BLOCK * (2 - a) : BLOCK * (3 - a)] = turned


def arrange_weight(pieces, spots):
    return call(
        functools.partial(arrange_body, spots), [shape((ROWS, COLS))] * 2, [], [], pieces, 0
    )


def edges():
    cell = lax.broadcasted_iota(jnp.int32, (1, FLAT), 1)
    col = cell % SIDE
    return cell, col


def fill(slab, refs, field):
    for p in range(PLANES):
        for m, ref in enumerate(refs[:SLOTS]):
            at = BLOCK * (p + 1) + PIECE * m
            field[at : at + PIECE, :] = ref[p]
    off, core = (ref[...].reshape(BLOCK, FLAT) for ref in refs[SLOTS:])
    off = jnp.where((slab == 0) | (slab == 15), jnp.zeros_like(off), off)
    odd = slab % 2 == 1
    field[:BLOCK, :] = jnp.where(odd, core, off)
    field[BLOCK * (PLANES + 1) :, :] = jnp.where(odd, off, core)


def conv_body(space_ref, weight_ref, *refs):
    own_ref, o1, o2, o3, field = refs[-5:]
    fill(space_ref[0], refs[:-5], field)
    cell, col = edges()
    weight = weight_ref[...]
    for d in range(PLANES):
        terms = jnp.dot(weight, field[BLOCK * d : BLOCK * d + COLS, :], preferred_element_type=F32)
        sums = []
        for c in range(3):
            up, mid, down = (terms[BLOCK * (3 * b + c) : BLOCK * (3 * b + c + 1)] for b in range(3))
            down = jnp.where(cell < FLAT - SIDE, pltpu.roll(down, FLAT - SIDE, 1), 0.0)
            up = jnp.where(cell >= SIDE, pltpu.roll(up, SIDE, 1), 0.0)
            sums.append(mid + down + up)
        left = jnp.where(col >= 1, pltpu.roll(sums[0], 1, 1), 0.0)
        right = jnp.where(col < SIDE - 1, pltpu.roll(sums[2], FLAT - 1, 1), 0.0)
        total = sums[1] + left + right
        own_ref[d] = total[:PIECE].astype(own_ref.dtype)
        for n, out in enumerate((o1, o2, o3), 1):
            out[d] = total[PIECE * n : PIECE * (n + 1)].astype(BF)


def conv(space, weight, slots):
    piece = (PLANES, PIECE, FLAT)
    return call(
        conv_body,
        [shape(piece, F32)] + [shape(piece)] * 3,
        [pltpu.VMEM((BLOCK * (PLANES + 2), FLAT), BF)],
        [space],
        [weight, *slots],
        2 * ROWS * COLS * FLAT * PLANES,
    )


def moves(err, cell, col):
    for c in range(3):
        if c == 0:
            one = jnp.where(col < SIDE - 1, pltpu.roll(err, FLAT - 1, 1), 0.0)
        elif c == 2:
            one = jnp.where(col >= 1, pltpu.roll(err, 1, 1), 0.0)
        else:
            one = err
        for b in range(3):
            if b == 0:
                two = jnp.where(cell < FLAT - SIDE, pltpu.roll(one, FLAT - SIDE, 1), 0.0)
            elif b == 2:
                two = jnp.where(cell >= SIDE, pltpu.roll(one, SIDE, 1), 0.0)
            else:
                two = one
            yield 3 * b + c, two.astype(BF)


def across(lhs, rhs):
    return lax.dot_general(lhs, rhs, (((1,), (1,)), ((), ())), preferred_element_type=F32)


def grad_body(spots, space_ref, *refs):
    slots, errs = refs[:6], refs[6:10]
    outs, (field, moved) = refs[10:-2], refs[-2:]
    fill(space_ref[0], slots, field)
    cell, col = edges()
    total = jnp.zeros((ROWS, COLS), F32)
    for d in range(PLANES):
        err = jnp.concatenate([e[d] for e in errs], axis=0).astype(F32)
        for q, two in moves(err, cell, col):
            for n in range(SLOTS):
                at = n * TALL + q * PIECE
                moved[at : at + PIECE, :] = two[PIECE * n : PIECE * (n + 1)]
        total = total + across(moved[...], field[BLOCK * d : BLOCK * d + COLS, :])
    for n in range(SLOTS):
        part = total[n * TALL : (n + 1) * TALL].astype(BF)
        out, at = outs[spots[n][0]], spots[n][1]
        end = at + GRAD_ROWS
        out[at : at + TALL, :] = part[:, : 2 * BLOCK]
        out[at + TALL : end, :BLOCK] = part[:SPLIT, 2 * BLOCK :]
        out[at + TALL : end - PIECE, BLOCK:] = part[SPLIT:, 2 * BLOCK :]
        out[end - PIECE : end, BLOCK:] = jnp.zeros((PIECE, BLOCK), BF)


def weight_grad(space, slots, errs, sent):
    return call(
        functools.partial(grad_body, sent),
        [shape((HALF * sum(k == j for k, _ in sent), LANES)) for j in range(1 + max(sent)[0])],
        [pltpu.VMEM((BLOCK * (PLANES + 2), FLAT), BF), pltpu.VMEM((ROWS, FLAT), BF)],
        [space],
        [*slots, *errs],
        2 * ROWS * COLS * FLAT * PLANES,
    )


def keep_body(space_ref, *refs):
    odd = space_ref[0] % 2 == 1
    pieces, (keep_ref, give_ref) = refs[:-2], refs[-2:]
    for n, (k, at) in enumerate(ARRIVED):
        first, second = pieces[n][...], pieces[SLOTS + k][at : at + GRAD_ROWS, :]
        rows = slice(n * GRAD_ROWS, (n + 1) * GRAD_ROWS)
        keep_ref[rows, :] = jnp.where(odd, second, first)
        give_ref[rows, :] = jnp.where(odd, first, second)


def fold_body(shift, count, space_ref, *refs):
    got, outs, held = refs[: -count - 1], refs[-count - 1 : -1], refs[-1]
    total = got[0][...].astype(F32)
    for ref in got[1:]:
        total = total + ref[...].astype(F32)
    held[...] = total
    part = outs[0].shape[0]
    at = (space_ref[0] >> shift) % count
    for m, out in enumerate(outs):
        out[...] = held[pl.ds(pl.multiple_of((at ^ m) * part, PIECE), part), :].astype(BF)


def fold(space, pieces, shift, count):
    rows = pieces[0].shape[0]
    return call(
        functools.partial(fold_body, shift, count),
        [shape((rows // count, LANES))] * count,
        [pltpu.VMEM((rows, LANES), F32)],
        [space],
        pieces,
        0,
    )


def join_body(shift, space_ref, *refs):
    out, count = refs[-1], len(refs) - 1
    part = refs[0].shape[0]
    at = (space_ref[0] >> shift) % count
    for m, ref in enumerate(refs[:-1]):
        out[pl.ds(pl.multiple_of((at ^ m) * part, PIECE), part), :] = ref[...]


def join(space, pieces, shift):
    rows = pieces[0].shape[0] * len(pieces)
    return call(
        functools.partial(join_body, shift), [shape((rows, LANES))], [], [space], pieces, 0
    )[0]


def finish_body(space_ref, chan_ref, mine_ref, got_ref, first_ref, second_ref):
    odd = space_ref[0] % 2 == 1
    first = jnp.where(odd, got_ref[...], mine_ref[...])
    second = jnp.where(odd, mine_ref[...], got_ref[...])
    for held, out, (take, give) in ((first, first_ref, FIRST), (second, second_ref, SECOND)):
        pick = chosen(chan_ref[0], take, give)
        for a in range(3):
            parts = []
            for n in range(SLOTS):
                at = n * GRAD_ROWS
                if a < 2:
                    parts.append(held[at : at + TALL, a * BLOCK : (a + 1) * BLOCK])
                else:
                    high = held[at + TALL : at + GRAD_ROWS, :BLOCK]
                    low = held[at + TALL : at + GRAD_ROWS - PIECE, BLOCK:]
                    parts.append(jnp.concatenate([high, low], axis=0))
            wide = jnp.concatenate(parts, axis=1)
            out[9 * a : 9 * (a + 1)] = across(wide, pick).reshape(9, PIECE, 256)


def finish(space, chan, mine, got):
    return call(
        finish_body,
        [shape((TAPS, PIECE, 256), F32)] * 2,
        [],
        [space, chan],
        [mine, got],
        2 * TAPS * PIECE * 256 * 256,
    )


def by_chan(array, mask):
    return lax.ppermute(array, "chan", [(i, i ^ mask) for i in range(16)]) if mask else array


def by_space(array, mask):
    return lax.ppermute(array, "space", [(i, i ^ mask) for i in range(16)])


def over_chan(arrays, masks):
    return [by_chan(array, mask) for array, mask in zip(arrays, masks)]


def gather(array, masks):
    return over_chan([array] * SLOTS, masks)


def borders(odd, slots):
    first = jnp.stack([s[0] for s in slots])
    last = jnp.stack([s[PLANES - 1] for s in slots])
    outward = [(i, (i + 1 if i % 2 else i - 1) % 16) for i in range(16)]
    off = lax.ppermute(jnp.where(odd, last, first), "space", outward)
    return [off, by_space(jnp.where(odd, first, last), 1)]


def add(pieces):
    total = pieces[0].astype(F32)
    for piece in pieces[1:]:
        total = total + piece.astype(F32)
    return total


def slope(value):
    sig = jax.nn.sigmoid(value)
    return sig * (1.0 + value * (1.0 - sig))


tie = lax.optimization_barrier


def shards(inputs, first_weight, second_weight, cotangent):
    space = lax.axis_index("space").astype(jnp.int32).reshape(1)
    chan = lax.axis_index("chan").astype(jnp.int32).reshape(1)
    odd = space[0] % 2 == 1
    inputs = inputs.transpose(1, 0, 2)
    cotangent = cotangent.transpose(1, 0, 2)

    in_slots = gather(inputs, FAR)
    in_slots[3], first_weight = tie((in_slots[3], first_weight))
    pieces = over_chan(split_weight(chan, first_weight, *FIRST, PLAIN), NEAR)
    in_slots, pieces = tie((in_slots, pieces))
    in_slots += borders(odd, in_slots)
    fwd_first, bwd_first = arrange_weight(pieces, PLAIN)
    more = split_weight(chan, second_weight, *SECOND, PASSED)
    in_slots, fwd_first, more = tie((in_slots, fwd_first, more))
    sums = over_chan(conv(space, fwd_first, in_slots), NEAR)
    one = by_chan(more[1], FAR[1])
    sums, one = tie((sums, one))
    pre_first = add(sums)
    hidden = jax.nn.silu(pre_first).astype(BF)

    hid_slots = gather(hidden, NEAR)
    two = by_chan(stitch(more[2], one), FAR[3])
    hid_slots, two = tie((hid_slots, two))
    hid_slots += borders(odd, hid_slots)
    fwd_second, bwd_second = arrange_weight([more[0], one, two], ARRIVED)
    pre_second = add(over_chan(conv(space, fwd_second, hid_slots), FAR))
    features = jax.nn.silu(pre_second).astype(BF)
    err_second = (cotangent.astype(F32) * slope(pre_second)).astype(BF)

    err2_slots = gather(err_second, FAR)
    parts = conv(space, bwd_second, err2_slots + borders(odd, err2_slots))
    err2_slots, parts = tie((err2_slots, parts))
    sums = over_chan(parts, NEAR)
    grads = weight_grad(space, hid_slots, err2_slots, PASSED)
    sums, grads = tie((sums, grads))
    grad_hidden = add(sums).astype(BF)
    err_first = (grad_hidden.astype(F32) * slope(pre_first)).astype(BF)

    err_first, grads = tie((err_first, grads))
    err1_slots = gather(err_first, NEAR)
    one = by_chan(grads[1], FAR[1])
    err1_slots, one = tie((err1_slots, one))
    firsts = weight_grad(space, in_slots, err1_slots, PLAIN)
    err1_slots, firsts, one = tie((err1_slots, firsts, one))
    firsts = over_chan(firsts, NEAR)
    two = by_chan(stitch(grads[2], one), FAR[3])
    err1_slots += borders(odd, err1_slots)
    firsts, two, err1_slots = tie((firsts, two, err1_slots))

    keep, give = call(
        keep_body, [shape((HELD, LANES))] * 2, [], [space], [*firsts, grads[0], one, two], 0
    )
    got, parts = tie((by_space(give, 1), conv(space, bwd_first, err1_slots)))
    mine, *rest = fold(space, [keep, got], 1, 4)
    rest = [by_space(r, 2 * m) for m, r in enumerate(rest, 1)]
    rest, near = tie((rest, by_chan(parts[1], FAR[1])))
    mine = fold(space, [mine, *rest], 0, 1)[0]
    got, side = tie((by_space(mine, 8), by_chan(parts[3], FAR[3])))
    mine = fold(space, [mine, got], 0, 1)[0]
    rest, far = tie(([by_space(mine, 2 * m) for m in (1, 2, 3)], by_chan(parts[2], FAR[2])))
    mine = join(space, [mine, *rest], 1)
    grad_first, grad_second = finish(space, chan, mine, by_space(mine, 1))
    grad_inputs = add([parts[0], near, far, side]).astype(BF)
    return (
        features.transpose(1, 0, 2),
        grad_first,
        grad_second,
        grad_inputs.transpose(1, 0, 2),
    )


def solution(mesh):
    slab = P("chan", "space", None)
    filters = P(None, "chan", None)
    return jax.shard_map(
        shards,
        mesh=mesh,
        in_specs=(slab, filters, filters, slab),
        out_specs=(slab, filters, filters, slab),
        check_vma=False,
    )
```

```python
import functools

import jax
import jax.numpy as jnp
import numpy as np
from jax import lax
from jax.experimental import pallas as pl
from jax.experimental.pallas import tpu as pltpu
from jax.sharding import PartitionSpec as P

SIDE = 32
FLAT = SIDE * SIDE
PLANES = 3
PIECE = 16
SLOTS = 4
BLOCK = SLOTS * PIECE
TAPS = 27
ROWS = 9 * BLOCK
COLS = 3 * BLOCK
NEAR = (0, 1, 2, 3)
FAR = (0, 8, 4, 12)
FIRST, SECOND = (FAR, NEAR), (NEAR, FAR)
LIMIT = 24 * 1024 * 1024
BF = jnp.bfloat16
F32 = jnp.float32


def call(body, outs, scratch, scalars, arrays, flops):
    moved = sum(int(np.prod(x.shape)) * x.dtype.itemsize for x in (*arrays, *outs))
    spec = pl.BlockSpec(memory_space=pltpu.VMEM)
    return pl.pallas_call(
        body,
        out_shape=outs,
        in_specs=[pl.BlockSpec(memory_space=pltpu.SMEM)] * len(scalars) + [spec] * len(arrays),
        out_specs=[spec] * len(outs),
        scratch_shapes=scratch,
        compiler_params=pltpu.CompilerParams(vmem_limit_bytes=LIMIT),
        cost_estimate=pl.CostEstimate(flops=flops, bytes_accessed=moved, transcendentals=0),
    )(*scalars, *arrays)


def shape(dims, dtype=BF):
    return jax.ShapeDtypeStruct(dims, dtype)


def chosen(chan, take, give):
    row = lax.broadcasted_iota(jnp.int32, (256, 256), 0)
    col = lax.broadcasted_iota(jnp.int32, (256, 256), 1)
    n, m = col // BLOCK, (col // PIECE) % SLOTS
    block = chan ^ (n % 2 * give[1]) ^ (n // 2 * give[2]) ^ (m % 2 * take[1]) ^ (m // 2 * take[2])
    return (row == block * PIECE + col % PIECE).astype(BF)


HALF = 14 * PIECE
TALL, SPLIT = 9 * PIECE, 5 * PIECE
GRAD_ROWS = TALL + SPLIT
HELD = SLOTS * GRAD_ROWS
PLAIN = ((0, 0), (1, 0), (2, 0), (3, 0))
PASSED = ((0, 0), (1, HALF), (1, 0), (2, 0))
ARRIVED = ((0, 0), (2, HALF), (1, 0), (2, 0))
LANES = 2 * BLOCK


def split_body(take, give, spots, chan_ref, weight_ref, *out_refs):
    pick = chosen(chan_ref[0], take, give)
    moved = jnp.dot(weight_ref[...], pick, preferred_element_type=F32).astype(BF)
    for n, (k, row) in enumerate(spots):
        part, out = moved[:, n * BLOCK : (n + 1) * BLOCK], out_refs[k]
        out[row : row + HALF, :BLOCK] = part[:HALF]
        out[row : row + HALF - PIECE, BLOCK:] = part[HALF:]
        out[row + HALF - PIECE : row + HALF, BLOCK:] = jnp.zeros((PIECE, BLOCK), BF)


def split_weight(chan, weight, take, give, sent):
    rows = TAPS * PIECE
    return call(
        functools.partial(split_body, take, give, sent),
        [shape((HALF * sum(k == j for k, _ in sent), LANES)) for j in range(1 + max(sent)[0])],
        [],
        [chan],
        [weight.reshape(rows, 256)],
        2 * rows * 256 * 256,
    )


def stitch_body(left_ref, right_ref, out_ref):
    out_ref[:HALF, :] = left_ref[...]
    out_ref[HALF:, :] = right_ref[HALF:, :]


def stitch(left, right):
    return call(stitch_body, [shape((2 * HALF, LANES))], [], [], [left, right], 0)[0]


def arrange_body(spots, *refs):
    fwd_ref, bwd_ref = refs[-2:]
    for a in range(3):
        for b in range(3):
            for c in range(3):
                k = 9 * a + 3 * b + c
                row, lane = PIECE * (k % 14), BLOCK * (k // 14)
                block = jnp.concatenate(
                    [refs[j][at + row : at + row + PIECE, lane : lane + BLOCK] for j, at in spots], axis=0
                )
                turned = block.astype(F32).T.astype(BF)
                at = COLS * b + BLOCK * a
                fwd_ref[BLOCK * c : BLOCK * (c + 1), at : at + BLOCK] = block
                at = COLS * (2 - b) + BLOCK * (2 - a)
                bwd_ref[BLOCK * (2 - c) : BLOCK * (3 - c), at : at + BLOCK] = turned


def arrange_weight(pieces, spots):
    return call(
        functools.partial(arrange_body, spots), [shape((COLS, ROWS))] * 2, [], [], pieces, 0
    )


def edges():
    cell = lax.broadcasted_iota(jnp.int32, (1, FLAT), 1)
    col = cell % SIDE
    return cell, col


def fill(slab, refs, field):
    for p in range(PLANES):
        for m, ref in enumerate(refs[:SLOTS]):
            at = BLOCK * (p + 1) + PIECE * m
            field[at : at + PIECE, :] = ref[p]
    off, core = (ref[...].reshape(BLOCK, FLAT) for ref in refs[SLOTS:])
    off = jnp.where((slab == 0) | (slab == 15), jnp.zeros_like(off), off)
    odd = slab % 2 == 1
    field[:BLOCK, :] = jnp.where(odd, core, off)
    field[BLOCK * (PLANES + 1) :, :] = jnp.where(odd, off, core)


def lift(rows, shift, cell):
    moved = pltpu.roll(rows, -shift % FLAT, 1)
    if shift > 0:
        end = jnp.where(cell[:, -LANES:] < FLAT - SIDE, moved[:, -LANES:], 0.0)
        return jnp.concatenate([moved[:, :-LANES], end], axis=1)
    end = jnp.where(cell[:, :LANES] >= SIDE, moved[:, :LANES], 0.0)
    return jnp.concatenate([end, moved[:, LANES:]], axis=1)


def conv_body(space_ref, weight_ref, *refs):
    own_ref, o1, o2, o3, up, field, down = refs[-7:]
    fill(space_ref[0], refs[:-7], field)
    cell, col = edges()
    for p in range(PLANES + 2):
        plane = slice(BLOCK * p, BLOCK * (p + 1))
        rows = field[plane, :].astype(F32)
        down[plane, :] = lift(rows, SIDE, cell).astype(BF)
        up[plane, :] = lift(rows, -SIDE, cell).astype(BF)
    weight = weight_ref[...]
    for d in range(PLANES):
        window = slice(BLOCK * d, BLOCK * d + COLS)
        terms = sum(
            jnp.dot(weight[:, COLS * b : COLS * (b + 1)], rows[window, :], preferred_element_type=F32)
            for b, rows in enumerate((up, field, down))
        )
        left, mid, right = (terms[BLOCK * c : BLOCK * (c + 1)] for c in range(3))
        left = jnp.where(col >= 1, pltpu.roll(left, 1, 1), 0.0)
        right = jnp.where(col < SIDE - 1, pltpu.roll(right, FLAT - 1, 1), 0.0)
        total = mid + left + right
        own_ref[d] = total[:PIECE]
        for n, out in enumerate((o1, o2, o3), 1):
            out[d] = total[PIECE * n : PIECE * (n + 1)].astype(BF)


def conv(space, weight, slots):
    piece = (PLANES, PIECE, FLAT)
    return call(
        conv_body,
        [shape(piece, F32)] + [shape(piece)] * 3,
        [pltpu.VMEM((BLOCK * (PLANES + 2), FLAT), BF)] * 3,
        [space],
        [weight, *slots],
        2 * ROWS * COLS * FLAT * PLANES,
    )


def moves(err, cell, col):
    for c in range(3):
        if c == 0:
            one = jnp.where(col < SIDE - 1, pltpu.roll(err, FLAT - 1, 1), 0.0)
        elif c == 2:
            one = jnp.where(col >= 1, pltpu.roll(err, 1, 1), 0.0)
        else:
            one = err
        for b in range(3):
            if b == 0:
                two = jnp.where(cell < FLAT - SIDE, pltpu.roll(one, FLAT - SIDE, 1), 0.0)
            elif b == 2:
                two = jnp.where(cell >= SIDE, pltpu.roll(one, SIDE, 1), 0.0)
            else:
                two = one
            yield 3 * b + c, two.astype(BF)


def across(lhs, rhs):
    return lax.dot_general(lhs, rhs, (((1,), (1,)), ((), ())), preferred_element_type=F32)


def grad_body(spots, space_ref, *refs):
    slots, errs = refs[:6], refs[6:10]
    outs, (field, moved, total) = refs[10:-3], refs[-3:]
    fill(space_ref[0], slots, field)
    cell, col = edges()
    total[...] = jnp.zeros((ROWS, COLS), F32)

    @pl.loop(0, PLANES)
    def _(d):
        err = jnp.concatenate([e[d] for e in errs], axis=0).astype(F32)
        for q, two in moves(err, cell, col):
            for n in range(SLOTS):
                at = n * TALL + q * PIECE
                moved[at : at + PIECE, :] = two[PIECE * n : PIECE * (n + 1)]
        rows = pl.ds(pl.multiple_of(BLOCK * d, BLOCK), COLS)
        total[...] += across(moved[...], field[rows, :])

    for n in range(SLOTS):
        part = total[n * TALL : (n + 1) * TALL, :].astype(BF)
        out, at = outs[spots[n][0]], spots[n][1]
        end = at + GRAD_ROWS
        out[at : at + TALL, :] = part[:, : 2 * BLOCK]
        out[at + TALL : end, :BLOCK] = part[:SPLIT, 2 * BLOCK :]
        out[at + TALL : end - PIECE, BLOCK:] = part[SPLIT:, 2 * BLOCK :]
        out[end - PIECE : end, BLOCK:] = jnp.zeros((PIECE, BLOCK), BF)


def weight_grad(space, slots, errs, sent):
    return call(
        functools.partial(grad_body, sent),
        [shape((HALF * sum(k == j for k, _ in sent), LANES)) for j in range(1 + max(sent)[0])],
        [
            pltpu.VMEM((BLOCK * (PLANES + 2), FLAT), BF),
            pltpu.VMEM((ROWS, FLAT), BF),
            pltpu.VMEM((ROWS, COLS), F32),
        ],
        [space],
        [*slots, *errs],
        2 * ROWS * COLS * FLAT * PLANES,
    )


def keep_body(space_ref, *refs):
    odd = space_ref[0] % 2 == 1
    pieces, (keep_ref, give_ref) = refs[:-2], refs[-2:]
    for n, (k, at) in enumerate(ARRIVED):
        first, second = pieces[n][...], pieces[SLOTS + k][at : at + GRAD_ROWS, :]
        rows = slice(n * GRAD_ROWS, (n + 1) * GRAD_ROWS)
        keep_ref[rows, :] = jnp.where(odd, second, first)
        give_ref[rows, :] = jnp.where(odd, first, second)


def total_body(*refs):
    terms = [ref[...].astype(F32) for ref in refs[:-1]]
    while len(terms) > 1:
        terms = [left + right for left, right in zip(terms[::2], terms[1::2])]
    refs[-1][...] = terms[0].astype(BF)


def total(pieces):
    return call(total_body, [shape((HELD, LANES))], [], [], pieces, 0)[0]


def finish_body(space_ref, chan_ref, mine_ref, got_ref, first_ref, second_ref):
    odd = space_ref[0] % 2 == 1
    first = jnp.where(odd, got_ref[...], mine_ref[...])
    second = jnp.where(odd, mine_ref[...], got_ref[...])
    for held, out, (take, give) in ((first, first_ref, FIRST), (second, second_ref, SECOND)):
        pick = chosen(chan_ref[0], take, give)
        for a in range(3):
            parts = []
            for n in range(SLOTS):
                at = n * GRAD_ROWS
                if a < 2:
                    parts.append(held[at : at + TALL, a * BLOCK : (a + 1) * BLOCK])
                else:
                    high = held[at + TALL : at + GRAD_ROWS, :BLOCK]
                    low = held[at + TALL : at + GRAD_ROWS - PIECE, BLOCK:]
                    parts.append(jnp.concatenate([high, low], axis=0))
            wide = jnp.concatenate(parts, axis=1)
            out[9 * a : 9 * (a + 1)] = across(wide, pick).reshape(9, PIECE, 256)


def finish(space, chan, mine, got):
    return call(
        finish_body,
        [shape((TAPS, PIECE, 256), F32)] * 2,
        [],
        [space, chan],
        [mine, got],
        2 * TAPS * PIECE * 256 * 256,
    )


def by_chan(array, mask):
    return lax.ppermute(array, "chan", [(i, i ^ mask) for i in range(16)]) if mask else array


def by_space(array, mask):
    return lax.ppermute(array, "space", [(i, i ^ mask) for i in range(16)])


def over_chan(arrays, masks):
    return [by_chan(array, mask) for array, mask in zip(arrays, masks)]


def gather(array, masks):
    return over_chan([array] * SLOTS, masks)


def edge_body(space_ref, s0, s1, s2, s3, off_ref, core_ref):
    odd = space_ref[0] % 2 == 1
    for m, ref in enumerate((s0, s1, s2, s3)):
        first, last = ref[0], ref[PLANES - 1]
        off_ref[m] = jnp.where(odd, last, first)
        core_ref[m] = jnp.where(odd, first, last)


def borders(space, slots):
    off, core = call(edge_body, [shape((SLOTS, PIECE, FLAT))] * 2, [], [space], slots, 0)
    outward = [(i, (i + 1 if i % 2 else i - 1) % 16) for i in range(16)]
    return [lax.ppermute(off, "space", outward), by_space(core, 1)]


def add(pieces):
    total = pieces[0].astype(F32)
    for piece in pieces[1:]:
        total = total + piece.astype(F32)
    return total


def slope(value):
    sig = jax.nn.sigmoid(value)
    return sig * (1.0 + value * (1.0 - sig))


tie = lax.optimization_barrier


def shards(inputs, first_weight, second_weight, cotangent):
    space = lax.axis_index("space").astype(jnp.int32).reshape(1)
    chan = lax.axis_index("chan").astype(jnp.int32).reshape(1)
    inputs = inputs.transpose(1, 0, 2)
    cotangent = cotangent.transpose(1, 0, 2)

    in_slots = gather(inputs, FAR)
    pieces = over_chan(split_weight(chan, first_weight, *FIRST, PLAIN), NEAR)
    more = split_weight(chan, second_weight, *SECOND, PASSED)
    in_slots, pieces, more = tie((in_slots, pieces, more))
    in_slots += borders(space, in_slots)
    fwd_first, bwd_first = arrange_weight(pieces, PLAIN)
    one = by_chan(more[1], FAR[2])
    in_slots, fwd_first = tie((in_slots, fwd_first))
    parts, one = tie((conv(space, fwd_first, in_slots), one))
    sums = over_chan(parts, NEAR)
    sums[1], one = tie((sums[1], one))
    two = by_chan(stitch(more[2], one), FAR[3])
    pre_first = add(sums)
    hidden = jax.nn.silu(pre_first).astype(BF)

    hid_slots = gather(hidden, NEAR)
    hid_slots, two = tie((hid_slots, two))
    hid_slots += borders(space, hid_slots)
    fwd_second, bwd_second = arrange_weight([more[0], one, two], ARRIVED)
    pre_second = add(over_chan(conv(space, fwd_second, hid_slots), FAR))
    features = jax.nn.silu(pre_second).astype(BF)
    err_second = (cotangent.astype(F32) * slope(pre_second)).astype(BF)

    err2_slots = gather(err_second, FAR)
    edge = borders(space, err2_slots)
    grads = weight_grad(space, hid_slots, err2_slots, PASSED)
    edge, grads = tie((edge, grads))
    parts, grads = tie((conv(space, bwd_second, err2_slots + edge), grads))
    sums = over_chan(parts, NEAR)
    one = by_chan(grads[1], FAR[2])
    sums, one = tie((sums, one))
    grad_hidden = add(sums).astype(BF)
    err_first = (grad_hidden.astype(F32) * slope(pre_first)).astype(BF)

    err1_slots = gather(err_first, NEAR)
    two = by_chan(stitch(grads[2], one), FAR[3])
    err1_slots, two = tie((err1_slots, two))
    firsts = over_chan(weight_grad(space, in_slots, err1_slots, PLAIN), NEAR)
    edge = borders(space, err1_slots)
    firsts, edge = tie((firsts, edge))
    keep, give = call(
        keep_body, [shape((HELD, LANES))] * 2, [], [space], [*firsts, grads[0], one, two], 0
    )
    got, parts = tie((by_space(give, 1), conv(space, bwd_first, err1_slots + edge)))
    mine, parts = tie((total([keep, got]), parts))
    got, far = tie((by_space(mine, 8), by_chan(parts[1], FAR[1])))
    mine = total([mine, got])
    mine, parts = tie((mine, parts))
    rest = [by_space(mine, 2 * m) for m in (1, 2, 3)]
    rest, near, side = tie((rest, by_chan(parts[2], FAR[2]), by_chan(parts[3], FAR[3])))
    mine = total([mine, *rest])
    grad_first, grad_second = finish(space, chan, mine, by_space(mine, 1))
    grad_inputs = add([parts[0], near, far, side]).astype(BF)
    return (
        features.transpose(1, 0, 2),
        grad_first,
        grad_second,
        grad_inputs.transpose(1, 0, 2),
    )


def solution(mesh):
    slab = P("chan", "space", None)
    filters = P(None, "chan", None)
    return jax.shard_map(
        shards,
        mesh=mesh,
        in_specs=(slab, filters, filters, slab),
        out_specs=(slab, filters, filters, slab),
        check_vma=False,
    )
```

```python
import functools

import jax
import jax.numpy as jnp
import numpy as np
from jax import lax
from jax.experimental import pallas as pl
from jax.experimental.pallas import tpu as pltpu
from jax.sharding import PartitionSpec as P

SIDE = 32
FLAT = SIDE * SIDE
PLANES = 3
PIECE = 16
SLOTS = 4
BLOCK = SLOTS * PIECE
TAPS = 27
ROWS = 9 * BLOCK
COLS = 3 * BLOCK
NEAR = (0, 1, 2, 3)
FAR = (0, 8, 4, 12)
FIRST, SECOND = (FAR, NEAR), (NEAR, FAR)
LIMIT = 24 * 1024 * 1024
BF = jnp.bfloat16
F32 = jnp.float32


def call(body, outs, scratch, scalars, arrays, flops):
    moved = sum(int(np.prod(x.shape)) * x.dtype.itemsize for x in (*arrays, *outs))
    spec = pl.BlockSpec(memory_space=pltpu.VMEM)
    return pl.pallas_call(
        body,
        out_shape=outs,
        in_specs=[pl.BlockSpec(memory_space=pltpu.SMEM)] * len(scalars) + [spec] * len(arrays),
        out_specs=[spec] * len(outs),
        scratch_shapes=scratch,
        compiler_params=pltpu.CompilerParams(vmem_limit_bytes=LIMIT),
        cost_estimate=pl.CostEstimate(flops=flops, bytes_accessed=moved, transcendentals=0),
    )(*scalars, *arrays)


def shape(dims, dtype=BF):
    return jax.ShapeDtypeStruct(dims, dtype)


def chosen(chan, take, give):
    row = lax.broadcasted_iota(jnp.int32, (256, 256), 0)
    col = lax.broadcasted_iota(jnp.int32, (256, 256), 1)
    n, m = col // BLOCK, (col // PIECE) % SLOTS
    block = chan ^ (n % 2 * give[1]) ^ (n // 2 * give[2]) ^ (m % 2 * take[1]) ^ (m // 2 * take[2])
    return (row == block * PIECE + col % PIECE).astype(BF)


HALF = 14 * PIECE
TALL, SPLIT = 9 * PIECE, 5 * PIECE
GRAD_ROWS = TALL + SPLIT
HELD = SLOTS * GRAD_ROWS
PLAIN = ((0, 0), (1, 0), (2, 0), (3, 0))
PASSED = ((0, 0), (1, HALF), (1, 0), (2, 0))
ARRIVED = ((0, 0), (2, HALF), (1, 0), (2, 0))
LANES = 2 * BLOCK


def split_body(take, give, spots, chan_ref, weight_ref, *out_refs):
    pick = chosen(chan_ref[0], take, give)
    moved = jnp.dot(weight_ref[...], pick, preferred_element_type=F32).astype(BF)
    for n, (k, row) in enumerate(spots):
        part, out = moved[:, n * BLOCK : (n + 1) * BLOCK], out_refs[k]
        out[row : row + HALF, :BLOCK] = part[:HALF]
        out[row : row + HALF - PIECE, BLOCK:] = part[HALF:]
        out[row + HALF - PIECE : row + HALF, BLOCK:] = jnp.zeros((PIECE, BLOCK), BF)


def split_weight(chan, weight, take, give, sent):
    rows = TAPS * PIECE
    return call(
        functools.partial(split_body, take, give, sent),
        [shape((HALF * sum(k == j for k, _ in sent), LANES)) for j in range(1 + max(sent)[0])],
        [],
        [chan],
        [weight.reshape(rows, 256)],
        2 * rows * 256 * 256,
    )


def stitch_body(left_ref, right_ref, out_ref):
    out_ref[:HALF, :] = left_ref[...]
    out_ref[HALF:, :] = right_ref[HALF:, :]


def stitch(left, right):
    return call(stitch_body, [shape((2 * HALF, LANES))], [], [], [left, right], 0)[0]


def arrange_body(spots, *refs):
    fwd_ref, bwd_ref = refs[-2:]
    for a in range(3):
        for b in range(3):
            for c in range(3):
                k = 9 * a + 3 * b + c
                row, lane = PIECE * (k % 14), BLOCK * (k // 14)
                block = jnp.concatenate(
                    [refs[j][at + row : at + row + PIECE, lane : lane + BLOCK] for j, at in spots], axis=0
                )
                turned = block.astype(F32).T.astype(BF)
                at = COLS * b + BLOCK * a
                fwd_ref[BLOCK * c : BLOCK * (c + 1), at : at + BLOCK] = block
                at = COLS * (2 - b) + BLOCK * (2 - a)
                bwd_ref[BLOCK * (2 - c) : BLOCK * (3 - c), at : at + BLOCK] = turned


def arrange_weight(pieces, spots):
    return call(
        functools.partial(arrange_body, spots), [shape((COLS, ROWS))] * 2, [], [], pieces, 0
    )


def edges():
    cell = lax.broadcasted_iota(jnp.int32, (1, FLAT), 1)
    col = cell % SIDE
    return cell, col


def fill(slab, refs, field):
    for p in range(PLANES):
        for m, ref in enumerate(refs[:SLOTS]):
            at = BLOCK * (p + 1) + PIECE * m
            field[at : at + PIECE, :] = ref[p]
    off, core = (ref[...].reshape(BLOCK, FLAT) for ref in refs[SLOTS:])
    off = jnp.where((slab == 0) | (slab == 15), jnp.zeros_like(off), off)
    odd = slab % 2 == 1
    field[:BLOCK, :] = jnp.where(odd, core, off)
    field[BLOCK * (PLANES + 1) :, :] = jnp.where(odd, off, core)


def lift(rows, shift, cell):
    moved = pltpu.roll(rows, -shift % FLAT, 1)
    if shift > 0:
        end = jnp.where(cell[:, -LANES:] < FLAT - SIDE, moved[:, -LANES:], 0.0)
        return jnp.concatenate([moved[:, :-LANES], end], axis=1)
    end = jnp.where(cell[:, :LANES] >= SIDE, moved[:, :LANES], 0.0)
    return jnp.concatenate([end, moved[:, LANES:]], axis=1)


def conv_body(space_ref, weight_ref, *refs):
    own_ref, o1, o2, o3, up, field, down = refs[-7:]
    fill(space_ref[0], refs[:-7], field)
    cell, col = edges()
    for p in range(PLANES + 2):
        plane = slice(BLOCK * p, BLOCK * (p + 1))
        rows = field[plane, :].astype(F32)
        down[plane, :] = lift(rows, SIDE, cell).astype(BF)
        up[plane, :] = lift(rows, -SIDE, cell).astype(BF)
    weight = weight_ref[...]
    for d in range(PLANES):
        window = slice(BLOCK * d, BLOCK * d + COLS)
        terms = sum(
            jnp.dot(weight[:, COLS * b : COLS * (b + 1)], rows[window, :], preferred_element_type=F32)
            for b, rows in enumerate((up, field, down))
        )
        left, mid, right = (terms[BLOCK * c : BLOCK * (c + 1)] for c in range(3))
        left = jnp.where(col >= 1, pltpu.roll(left, 1, 1), 0.0)
        right = jnp.where(col < SIDE - 1, pltpu.roll(right, FLAT - 1, 1), 0.0)
        total = mid + left + right
        own_ref[d] = total[:PIECE]
        for n, out in enumerate((o1, o2, o3), 1):
            out[d] = total[PIECE * n : PIECE * (n + 1)].astype(BF)


def conv(space, weight, slots):
    piece = (PLANES, PIECE, FLAT)
    return call(
        conv_body,
        [shape(piece, F32)] + [shape(piece)] * 3,
        [pltpu.VMEM((BLOCK * (PLANES + 2), FLAT), BF)] * 3,
        [space],
        [weight, *slots],
        2 * ROWS * COLS * FLAT * PLANES,
    )


def moves(err, cell, col):
    for c in range(3):
        if c == 0:
            one = jnp.where(col < SIDE - 1, pltpu.roll(err, FLAT - 1, 1), 0.0)
        elif c == 2:
            one = jnp.where(col >= 1, pltpu.roll(err, 1, 1), 0.0)
        else:
            one = err
        for b in range(3):
            if b == 0:
                two = jnp.where(cell < FLAT - SIDE, pltpu.roll(one, FLAT - SIDE, 1), 0.0)
            elif b == 2:
                two = jnp.where(cell >= SIDE, pltpu.roll(one, SIDE, 1), 0.0)
            else:
                two = one
            yield 3 * b + c, two.astype(BF)


def across(lhs, rhs):
    return lax.dot_general(lhs, rhs, (((1,), (1,)), ((), ())), preferred_element_type=F32)


def grad_body(spots, space_ref, *refs):
    slots, errs = refs[:6], refs[6:10]
    outs, (field, moved, total) = refs[10:-3], refs[-3:]
    fill(space_ref[0], slots, field)
    cell, col = edges()
    total[...] = jnp.zeros((ROWS, COLS), F32)

    @pl.loop(0, PLANES)
    def _(d):
        err = jnp.concatenate([e[d] for e in errs], axis=0).astype(F32)
        for q, two in moves(err, cell, col):
            for n in range(SLOTS):
                at = n * TALL + q * PIECE
                moved[at : at + PIECE, :] = two[PIECE * n : PIECE * (n + 1)]
        rows = pl.ds(pl.multiple_of(BLOCK * d, BLOCK), COLS)
        total[...] += across(moved[...], field[rows, :])

    for n in range(SLOTS):
        part = total[n * TALL : (n + 1) * TALL, :].astype(BF)
        out, at = outs[spots[n][0]], spots[n][1]
        end = at + GRAD_ROWS
        out[at : at + TALL, :] = part[:, : 2 * BLOCK]
        out[at + TALL : end, :BLOCK] = part[:SPLIT, 2 * BLOCK :]
        out[at + TALL : end - PIECE, BLOCK:] = part[SPLIT:, 2 * BLOCK :]
        out[end - PIECE : end, BLOCK:] = jnp.zeros((PIECE, BLOCK), BF)


def weight_grad(space, slots, errs, sent):
    return call(
        functools.partial(grad_body, sent),
        [shape((HALF * sum(k == j for k, _ in sent), LANES)) for j in range(1 + max(sent)[0])],
        [
            pltpu.VMEM((BLOCK * (PLANES + 2), FLAT), BF),
            pltpu.VMEM((ROWS, FLAT), BF),
            pltpu.VMEM((ROWS, COLS), F32),
        ],
        [space],
        [*slots, *errs],
        2 * ROWS * COLS * FLAT * PLANES,
    )


def keep_body(space_ref, *refs):
    odd = space_ref[0] % 2 == 1
    pieces, (keep_ref, give_ref) = refs[:-2], refs[-2:]
    for n, (k, at) in enumerate(ARRIVED):
        first, second = pieces[n][...], pieces[SLOTS + k][at : at + GRAD_ROWS, :]
        rows = slice(n * GRAD_ROWS, (n + 1) * GRAD_ROWS)
        keep_ref[rows, :] = jnp.where(odd, second, first)
        give_ref[rows, :] = jnp.where(odd, first, second)


def total_body(*refs):
    terms = [ref[...].astype(F32) for ref in refs[:-1]]
    while len(terms) > 1:
        terms = [left + right for left, right in zip(terms[::2], terms[1::2])]
    refs[-1][...] = terms[0].astype(BF)


def total(pieces):
    return call(total_body, [shape((HELD, LANES))], [], [], pieces, 0)[0]


def finish_body(space_ref, chan_ref, mine_ref, got_ref, first_ref, second_ref):
    odd = space_ref[0] % 2 == 1
    first = jnp.where(odd, got_ref[...], mine_ref[...])
    second = jnp.where(odd, mine_ref[...], got_ref[...])
    for held, out, (take, give) in ((first, first_ref, FIRST), (second, second_ref, SECOND)):
        pick = chosen(chan_ref[0], take, give)
        for a in range(3):
            parts = []
            for n in range(SLOTS):
                at = n * GRAD_ROWS
                if a < 2:
                    parts.append(held[at : at + TALL, a * BLOCK : (a + 1) * BLOCK])
                else:
                    high = held[at + TALL : at + GRAD_ROWS, :BLOCK]
                    low = held[at + TALL : at + GRAD_ROWS - PIECE, BLOCK:]
                    parts.append(jnp.concatenate([high, low], axis=0))
            wide = jnp.concatenate(parts, axis=1)
            out[9 * a : 9 * (a + 1)] = across(wide, pick).reshape(9, PIECE, 256)


def finish(space, chan, mine, got):
    return call(
        finish_body,
        [shape((TAPS, PIECE, 256), F32)] * 2,
        [],
        [space, chan],
        [mine, got],
        2 * TAPS * PIECE * 256 * 256,
    )


def by_chan(array, mask):
    return lax.ppermute(array, "chan", [(i, i ^ mask) for i in range(16)]) if mask else array


def by_space(array, mask):
    return lax.ppermute(array, "space", [(i, i ^ mask) for i in range(16)])


def over_chan(arrays, masks):
    return [by_chan(array, mask) for array, mask in zip(arrays, masks)]


def gather(array, masks):
    return over_chan([array] * SLOTS, masks)


def edge_body(cross, space_ref, s0, s1, s2, s3, off_ref, core_ref):
    slab = space_ref[0]
    odd, middle = slab % 2 == 1, (slab == 7) | (slab == 8)
    slots = (s0, s1, s2, s3)
    for m, ref in enumerate(slots):
        first, last = ref[0], ref[PLANES - 1]
        outer = jnp.where(odd, last, first)
        if cross:
            peer = slots[m ^ 1]
            outer = jnp.where(middle, jnp.where(odd, peer[PLANES - 1], peer[0]), outer)
        off_ref[m] = outer
        core_ref[m] = jnp.where(odd, first, last)


def outward(slab, chan, cross):
    if slab in (0, 15):
        return 16 * slab + (chan ^ 1)
    there = slab + 1 if slab % 2 else slab - 1
    return 16 * there + (chan ^ (cross and slab in (7, 8)))


def borders(space, slots, cross):
    body = functools.partial(edge_body, cross)
    off, core = call(body, [shape((SLOTS, PIECE, FLAT))] * 2, [], [space], slots, 0)
    pairs = [(16 * i + c, outward(i, c, cross)) for i in range(16) for c in range(16)]
    return [lax.ppermute(off, ("space", "chan"), pairs), by_space(core, 1)]


def add(pieces):
    total = pieces[0].astype(F32)
    for piece in pieces[1:]:
        total = total + piece.astype(F32)
    return total


def slope(value):
    sig = jax.nn.sigmoid(value)
    return sig * (1.0 + value * (1.0 - sig))


tie = lax.optimization_barrier


def shards(inputs, first_weight, second_weight, cotangent):
    space = lax.axis_index("space").astype(jnp.int32).reshape(1)
    chan = lax.axis_index("chan").astype(jnp.int32).reshape(1)
    inputs = inputs.transpose(1, 0, 2)
    cotangent = cotangent.transpose(1, 0, 2)

    in_slots = gather(inputs, FAR)
    pieces = over_chan(split_weight(chan, first_weight, *FIRST, PLAIN), NEAR)
    more = split_weight(chan, second_weight, *SECOND, PASSED)
    in_slots, pieces, more = tie((in_slots, pieces, more))
    in_slots += borders(space, in_slots, False)
    fwd_first, bwd_first = arrange_weight(pieces, PLAIN)
    one = by_chan(more[1], FAR[2])
    in_slots, fwd_first = tie((in_slots, fwd_first))
    sums = over_chan(conv(space, fwd_first, in_slots), NEAR)
    sums[1], one = tie((sums[1], one))
    two = by_chan(stitch(more[2], one), FAR[3])
    pre_first = add(sums)
    hidden = jax.nn.silu(pre_first).astype(BF)

    hid_slots = gather(hidden, NEAR)
    hid_slots, two = tie((hid_slots, two))
    hid_slots += borders(space, hid_slots, True)
    fwd_second, bwd_second = arrange_weight([more[0], one, two], ARRIVED)
    pre_second = add(over_chan(conv(space, fwd_second, hid_slots), FAR))
    features = jax.nn.silu(pre_second).astype(BF)
    err_second = (cotangent.astype(F32) * slope(pre_second)).astype(BF)

    err2_slots = gather(err_second, FAR)
    edge = borders(space, err2_slots, False)
    grads = weight_grad(space, hid_slots, err2_slots, PASSED)
    edge, grads = tie((edge, grads))
    sums = over_chan(conv(space, bwd_second, err2_slots + edge), NEAR)
    one = by_chan(grads[1], FAR[2])
    sums, one = tie((sums, one))
    grad_hidden = add(sums).astype(BF)
    err_first = (grad_hidden.astype(F32) * slope(pre_first)).astype(BF)

    err1_slots = gather(err_first, NEAR)
    two = by_chan(stitch(grads[2], one), FAR[3])
    err1_slots, two = tie((err1_slots, two))
    firsts, err1_slots = tie((weight_grad(space, in_slots, err1_slots, PLAIN), err1_slots))
    firsts = over_chan(firsts, NEAR)
    edge = borders(space, err1_slots, True)
    firsts, edge = tie((firsts, edge))
    keep, give = call(
        keep_body, [shape((HELD, LANES))] * 2, [], [space], [*firsts, grads[0], one, two], 0
    )
    got, parts = tie((by_space(give, 1), conv(space, bwd_first, err1_slots + edge)))
    mine, parts = tie((total([keep, got]), parts))
    got, near = tie((by_space(mine, 8), by_chan(parts[2], FAR[2])))
    mine = total([mine, got])
    mine, parts = tie((mine, parts))
    rest = [by_space(mine, 2 * m) for m in (1, 2, 3)]
    rest, far, side = tie((rest, by_chan(parts[1], FAR[1]), by_chan(parts[3], FAR[3])))
    mine = total([mine, *rest])
    grad_first, grad_second = finish(space, chan, mine, by_space(mine, 1))
    grad_inputs = add([parts[0], near, far, side]).astype(BF)
    return (
        features.transpose(1, 0, 2),
        grad_first,
        grad_second,
        grad_inputs.transpose(1, 0, 2),
    )


def solution(mesh):
    slab = P("chan", "space", None)
    filters = P(None, "chan", None)
    return jax.shard_map(
        shards,
        mesh=mesh,
        in_specs=(slab, filters, filters, slab),
        out_specs=(slab, filters, filters, slab),
        check_vma=False,
    )
```

```python
import functools

import jax
import jax.numpy as jnp
import numpy as np
from jax import lax
from jax.experimental import pallas as pl
from jax.experimental.pallas import tpu as pltpu
from jax.sharding import PartitionSpec as P

SIDE = 32
FLAT = SIDE * SIDE
PLANES = 3
PIECE = 16
SLOTS = 4
BLOCK = SLOTS * PIECE
TAPS = 27
ROWS = 9 * BLOCK
COLS = 3 * BLOCK
NEAR = (0, 1, 2, 3)
FAR = (0, 8, 4, 12)
FIRST, SECOND = (FAR, NEAR), (NEAR, FAR)
LIMIT = 24 * 1024 * 1024
BF = jnp.bfloat16
F32 = jnp.float32


def call(body, outs, scratch, scalars, arrays, flops):
    moved = sum(int(np.prod(x.shape)) * x.dtype.itemsize for x in (*arrays, *outs))
    spec = pl.BlockSpec(memory_space=pltpu.VMEM)
    return pl.pallas_call(
        body,
        out_shape=outs,
        in_specs=[pl.BlockSpec(memory_space=pltpu.SMEM)] * len(scalars) + [spec] * len(arrays),
        out_specs=[spec] * len(outs),
        scratch_shapes=scratch,
        compiler_params=pltpu.CompilerParams(vmem_limit_bytes=LIMIT),
        cost_estimate=pl.CostEstimate(flops=flops, bytes_accessed=moved, transcendentals=0),
    )(*scalars, *arrays)


def shape(dims, dtype=BF):
    return jax.ShapeDtypeStruct(dims, dtype)


def chosen(chan, take, give):
    row = lax.broadcasted_iota(jnp.int32, (256, 256), 0)
    col = lax.broadcasted_iota(jnp.int32, (256, 256), 1)
    n, m = col // BLOCK, (col // PIECE) % SLOTS
    block = chan ^ (n % 2 * give[1]) ^ (n // 2 * give[2]) ^ (m % 2 * take[1]) ^ (m // 2 * take[2])
    return (row == block * PIECE + col % PIECE).astype(BF)


HALF = 14 * PIECE
GRAD_ROWS = 14 * PIECE
HELD = SLOTS * GRAD_ROWS
PLAIN = ((0, 0), (1, 0), (2, 0), (3, 0))
PASSED = ((0, 0), (1, HALF), (1, 0), (2, 0))
ARRIVED = ((0, 0), (2, HALF), (1, 0), (2, 0))
LANES = 2 * BLOCK


def split_body(take, give, spots, chan_ref, weight_ref, *out_refs):
    pick = chosen(chan_ref[0], take, give)
    moved = jnp.dot(weight_ref[...], pick, preferred_element_type=F32).astype(BF)
    for n, (k, row) in enumerate(spots):
        part, out = moved[:, n * BLOCK : (n + 1) * BLOCK], out_refs[k]
        out[row : row + HALF, :BLOCK] = part[:HALF]
        out[row : row + HALF - PIECE, BLOCK:] = part[HALF:]
        out[row + HALF - PIECE : row + HALF, BLOCK:] = jnp.zeros((PIECE, BLOCK), BF)


def split_weight(chan, weight, take, give, sent):
    rows = TAPS * PIECE
    return call(
        functools.partial(split_body, take, give, sent),
        [shape((HALF * sum(k == j for k, _ in sent), LANES)) for j in range(1 + max(sent)[0])],
        [],
        [chan],
        [weight.reshape(rows, 256)],
        2 * rows * 256 * 256,
    )


def stitch_body(left_ref, right_ref, out_ref):
    out_ref[:HALF, :] = left_ref[...]
    out_ref[HALF:, :] = right_ref[HALF:, :]


def stitch(left, right):
    return call(stitch_body, [shape((2 * HALF, LANES))], [], [], [left, right], 0)[0]


def arrange_body(spots, *refs):
    for a in range(3):
        for b in range(3):
            for c in range(3):
                k = 9 * a + 3 * b + c
                row, lane = PIECE * (k % 14), BLOCK * (k // 14)
                block = jnp.concatenate(
                    [refs[j][at + row : at + row + PIECE, lane : lane + BLOCK] for j, at in spots], axis=0
                )
                at = COLS * b + BLOCK * a
                refs[-1][BLOCK * c : BLOCK * (c + 1), at : at + BLOCK] = block


def arrange_weight(pieces, spots):
    return call(
        functools.partial(arrange_body, spots), [shape((COLS, ROWS))], [], [], pieces, 0
    )[0]


def turn_body(fwd_ref, bwd_ref):
    for a in range(3):
        for b in range(3):

            @pl.loop(0, 3)
            def _(c):
                here = pl.ds(pl.multiple_of(BLOCK * c, BLOCK), BLOCK)
                there = pl.ds(pl.multiple_of(BLOCK * (2 - c), BLOCK), BLOCK)
                at, to = COLS * b + BLOCK * a, COLS * (2 - b) + BLOCK * (2 - a)
                block = fwd_ref[here, at : at + BLOCK].astype(F32)
                bwd_ref[there, to : to + BLOCK] = block.T.astype(BF)


def turn_weight(weight):
    return call(turn_body, [shape((COLS, ROWS))], [], [], [weight], 0)[0]


def edges():
    cell = lax.broadcasted_iota(jnp.int32, (1, FLAT), 1)
    col = cell % SIDE
    return cell, col


def fill(slab, refs, field):
    for p in range(PLANES):
        for m, ref in enumerate(refs[:SLOTS]):
            at = BLOCK * (p + 1) + PIECE * m
            field[at : at + PIECE, :] = ref[p]
    off, core = (ref[...].reshape(BLOCK, FLAT) for ref in refs[SLOTS:])
    off = jnp.where((slab == 0) | (slab == 15), jnp.zeros_like(off), off)
    odd = slab % 2 == 1
    field[:BLOCK, :] = jnp.where(odd, core, off)
    field[BLOCK * (PLANES + 1) :, :] = jnp.where(odd, off, core)


def lift(rows, shift, cell):
    moved = pltpu.roll(rows, -shift % FLAT, 1)
    if shift > 0:
        end = jnp.where(cell[:, -LANES:] < FLAT - SIDE, moved[:, -LANES:], 0.0)
        return jnp.concatenate([moved[:, :-LANES], end], axis=1)
    end = jnp.where(cell[:, :LANES] >= SIDE, moved[:, :LANES], 0.0)
    return jnp.concatenate([end, moved[:, LANES:]], axis=1)


def lift_one(p, up, field, down, cell):
    plane = pl.ds(pl.multiple_of(BLOCK * p, BLOCK), BLOCK)
    rows = field[plane, :].astype(F32)
    down[plane, :] = lift(rows, SIDE, cell).astype(BF)
    up[plane, :] = lift(rows, -SIDE, cell).astype(BF)


def conv_body(space_ref, weight_ref, *refs):
    own_ref, o1, o2, o3, up, field, down = refs[-7:]
    fill(space_ref[0], refs[:-7], field)
    cell, col = edges()
    for p in range(PLANES + 2):
        lift_one(p, up, field, down, cell)
    weight = weight_ref[...]
    for d in range(PLANES):
        window = slice(BLOCK * d, BLOCK * d + COLS)
        terms = sum(
            jnp.dot(weight[:, COLS * b : COLS * (b + 1)], rows[window, :], preferred_element_type=F32)
            for b, rows in enumerate((up, field, down))
        )
        left, mid, right = (terms[BLOCK * c : BLOCK * (c + 1)] for c in range(3))
        left = jnp.where(col >= 1, pltpu.roll(left, 1, 1), 0.0)
        right = jnp.where(col < SIDE - 1, pltpu.roll(right, FLAT - 1, 1), 0.0)
        total = mid + left + right
        own_ref[d] = total[:PIECE]
        for n, out in enumerate((o1, o2, o3), 1):
            out[d] = total[PIECE * n : PIECE * (n + 1)].astype(BF)


def conv(space, weight, slots):
    piece = (PLANES, PIECE, FLAT)
    return call(
        conv_body,
        [shape(piece, F32)] + [shape(piece)] * 3,
        [pltpu.VMEM((BLOCK * (PLANES + 2), FLAT), BF)] * 3,
        [space],
        [weight, *slots],
        2 * ROWS * COLS * FLAT * PLANES,
    )


def across(lhs, rhs):
    return lax.dot_general(lhs, rhs, (((1,), (1,)), ((), ())), preferred_element_type=F32)


def looped(count):
    return pl.loop(0, count)


def straight(count):
    return lambda step: [step(i) for i in range(count)]


def grad_body(spots, each, space_ref, *refs):
    slots, errs = refs[:6], refs[6:10]
    outs, (up, field, down, moved, total) = refs[10:-5], refs[-5:]
    fill(space_ref[0], slots, field)
    cell, col = edges()
    each(PLANES + 2)(lambda p: lift_one(p, up, field, down, cell))
    total[...] = jnp.zeros((COLS, ROWS), F32)

    @each(PLANES)
    def _(d):
        err = jnp.concatenate([e[d] for e in errs], axis=0)
        wide = err.astype(F32)
        left = jnp.where(col < SIDE - 1, pltpu.roll(wide, FLAT - 1, 1), 0.0)
        right = jnp.where(col >= 1, pltpu.roll(wide, 1, 1), 0.0)
        moved[:BLOCK, :] = left.astype(BF)
        moved[BLOCK : 2 * BLOCK, :] = err
        moved[2 * BLOCK :, :] = right.astype(BF)
        window = pl.ds(pl.multiple_of(BLOCK * d, BLOCK), COLS)
        for b, rows in enumerate((up, field, down)):
            part, at = across(moved[...], rows[window, :]), slice(COLS * b, COLS * (b + 1))
            total[:, at] += part
    for n, (k, at) in enumerate(spots):
        part = jnp.concatenate(
            [total[BLOCK * c + PIECE * n : BLOCK * c + PIECE * (n + 1), :] for c in range(3)], axis=0
        ).astype(BF)
        out = outs[k]
        for j in range(4):
            out[at + 48 * j : at + 48 * (j + 1), :] = part[:, LANES * j : LANES * (j + 1)]
        out[at + 192 : at + 224, :BLOCK] = part[:32, 4 * LANES :]
        out[at + 192 : at + 208, BLOCK:] = part[32:, 4 * LANES :]
        out[at + 208 : at + 224, BLOCK:] = jnp.zeros((PIECE, BLOCK), BF)


def weight_grad(space, slots, errs, sent, each):
    return call(
        functools.partial(grad_body, sent, each),
        [shape((HALF * sum(k == j for k, _ in sent), LANES)) for j in range(1 + max(sent)[0])],
        [pltpu.VMEM((BLOCK * (PLANES + 2), FLAT), BF)] * 3
        + [pltpu.VMEM((COLS, FLAT), BF), pltpu.VMEM((COLS, ROWS), F32)],
        [space],
        [*slots, *errs],
        2 * ROWS * COLS * FLAT * PLANES,
    )


def keep_body(space_ref, *refs):
    odd = space_ref[0] % 2 == 1
    pieces, (keep_ref, give_ref) = refs[:-2], refs[-2:]
    for n, (k, at) in enumerate(ARRIVED):

        @pl.loop(0, GRAD_ROWS, step=PIECE * 2)
        def _(i):
            here, there, rows = (
                pl.ds(pl.multiple_of(start + i, PIECE), PIECE * 2) for start in (0, at, n * GRAD_ROWS)
            )
            first, second = pieces[n][here, :], pieces[SLOTS + k][there, :]
            keep_ref[rows, :] = jnp.where(odd, second, first)
            give_ref[rows, :] = jnp.where(odd, first, second)


def total_body(*refs):
    @pl.loop(0, 7)
    def _(i):
        rows = pl.ds(pl.multiple_of(LANES * i, LANES), LANES)
        terms = [ref[rows, :].astype(F32) for ref in refs[:-1]]
        while len(terms) > 1:
            terms = [left + right for left, right in zip(terms[::2], terms[1::2])]
        refs[-1][rows, :] = terms[0].astype(BF)


def total(pieces):
    return call(total_body, [shape((HELD, LANES))], [], [], pieces, 0)[0]


def finish_body(space_ref, chan_ref, mine_ref, got_ref, first_ref, second_ref):
    odd = space_ref[0] % 2 == 1
    first = jnp.where(odd, got_ref[...], mine_ref[...])
    second = jnp.where(odd, mine_ref[...], got_ref[...])
    for held, out, (take, give) in ((first, first_ref, FIRST), (second, second_ref, SECOND)):
        pick = chosen(chan_ref[0], take, give)
        columns = []
        for n in range(SLOTS):
            at = n * GRAD_ROWS
            parts = [
                held[at + 48 * (j // 2) : at + 48 * (j // 2 + 1), BLOCK * (j % 2) : BLOCK * (j % 2 + 1)]
                for j in range(8)
            ]
            parts += [held[at + 192 : at + 224, :BLOCK], held[at + 192 : at + 208, BLOCK:]]
            columns.append(jnp.concatenate(parts, axis=0))
        back = across(jnp.concatenate(columns, axis=1), pick).reshape(TAPS, PIECE, 256)
        for j in range(9):
            k = 9 * (j % 3) + 3 * (j // 3)
            out[k : k + 3] = back[3 * j : 3 * j + 3]


def finish(space, chan, mine, got):
    return call(
        finish_body,
        [shape((TAPS, PIECE, 256), F32)] * 2,
        [],
        [space, chan],
        [mine, got],
        2 * TAPS * PIECE * 256 * 256,
    )


def by_chan(array, mask):
    return lax.ppermute(array, "chan", [(i, i ^ mask) for i in range(16)]) if mask else array


def by_space(array, mask):
    return lax.ppermute(array, "space", [(i, i ^ mask) for i in range(16)])


def over_chan(arrays, masks):
    return [by_chan(array, mask) for array, mask in zip(arrays, masks)]


def gather(array, masks):
    return over_chan([array] * SLOTS, masks)


def edge_body(cross, space_ref, s0, s1, s2, s3, off_ref, core_ref):
    slab = space_ref[0]
    odd, middle = slab % 2 == 1, (slab == 7) | (slab == 8)
    slots = (s0, s1, s2, s3)
    for m, ref in enumerate(slots):
        first, last = ref[0], ref[PLANES - 1]
        outer = jnp.where(odd, last, first)
        if cross:
            peer = slots[m ^ 1]
            outer = jnp.where(middle, jnp.where(odd, peer[PLANES - 1], peer[0]), outer)
        off_ref[m] = outer
        core_ref[m] = jnp.where(odd, first, last)


def outward(slab, chan, cross):
    if slab in (0, 15):
        return 16 * slab + (chan ^ 1)
    there = slab + 1 if slab % 2 else slab - 1
    return 16 * there + (chan ^ (cross and slab in (7, 8)))


def borders(space, slots, cross):
    body = functools.partial(edge_body, cross)
    off, core = call(body, [shape((SLOTS, PIECE, FLAT))] * 2, [], [space], slots, 0)
    pairs = [(16 * i + c, outward(i, c, cross)) for i in range(16) for c in range(16)]
    return [lax.ppermute(off, ("space", "chan"), pairs), by_space(core, 1)]


def add(pieces):
    total = pieces[0].astype(F32)
    for piece in pieces[1:]:
        total = total + piece.astype(F32)
    return total


def slope(value):
    sig = jax.nn.sigmoid(value)
    return sig * (1.0 + value * (1.0 - sig))


tie = lax.optimization_barrier


def shards(inputs, first_weight, second_weight, cotangent):
    space = lax.axis_index("space").astype(jnp.int32).reshape(1)
    chan = lax.axis_index("chan").astype(jnp.int32).reshape(1)
    inputs = inputs.transpose(1, 0, 2)
    cotangent = cotangent.transpose(1, 0, 2)

    in_slots = gather(inputs, FAR)
    pieces = over_chan(split_weight(chan, first_weight, *FIRST, PLAIN), NEAR)
    more = split_weight(chan, second_weight, *SECOND, PASSED)
    in_slots, pieces, more = tie((in_slots, pieces, more))
    in_slots += borders(space, in_slots, False)
    fwd_first = arrange_weight(pieces, PLAIN)
    one = by_chan(more[1], FAR[2])
    in_slots, fwd_first = tie((in_slots, fwd_first))
    sums = over_chan(conv(space, fwd_first, in_slots), NEAR)
    sums[1], one = tie((sums[1], one))
    two = by_chan(stitch(more[2], one), FAR[3])
    pre_first = add(sums)
    hidden = jax.nn.silu(pre_first).astype(BF)

    hid_slots = gather(hidden, NEAR)
    hid_slots, two = tie((hid_slots, two))
    hid_slots += borders(space, hid_slots, True)
    fwd_second = arrange_weight([more[0], one, two], ARRIVED)
    parts, fwd_second = tie((conv(space, fwd_second, hid_slots), fwd_second))
    sums, bwd_second = tie((over_chan(parts, FAR), turn_weight(fwd_second)))
    pre_second = add(sums)
    features = jax.nn.silu(pre_second).astype(BF)
    err_second = (cotangent.astype(F32) * slope(pre_second)).astype(BF)

    err_second, fwd_first = tie((err_second, fwd_first))
    err2_slots = gather(err_second, FAR)
    err2_slots, bwd_first = tie((err2_slots, turn_weight(fwd_first)))
    edge = borders(space, err2_slots, False)
    grads = weight_grad(space, hid_slots, err2_slots, PASSED, looped)
    edge, grads = tie((edge, grads))
    sums = over_chan(conv(space, bwd_second, err2_slots + edge), NEAR)
    one = by_chan(grads[1], FAR[2])
    sums, one = tie((sums, one))
    grad_hidden = add(sums).astype(BF)
    err_first = (grad_hidden.astype(F32) * slope(pre_first)).astype(BF)

    err1_slots = gather(err_first, NEAR)
    two = by_chan(stitch(grads[2], one), FAR[3])
    err1_slots, two = tie((err1_slots, two))
    firsts, err1_slots = tie((weight_grad(space, in_slots, err1_slots, PLAIN, straight), err1_slots))
    firsts = over_chan(firsts, NEAR)
    edge = borders(space, err1_slots, True)
    firsts, edge = tie((firsts, edge))
    keep, give = call(
        keep_body, [shape((HELD, LANES))] * 2, [], [space], [*firsts, grads[0], one, two], 0
    )
    got, parts = tie((by_space(give, 1), conv(space, bwd_first, err1_slots + edge)))
    mine, parts = tie((total([keep, got]), parts))
    got, near = tie((by_space(mine, 8), by_chan(parts[2], FAR[2])))
    mine = total([mine, got])
    mine, parts = tie((mine, parts))
    rest = [by_space(mine, 2 * m) for m in (1, 2, 3)]
    rest, far, side = tie((rest, by_chan(parts[1], FAR[1]), by_chan(parts[3], FAR[3])))
    mine = total([mine, *rest])
    grad_first, grad_second = finish(space, chan, mine, by_space(mine, 1))
    grad_inputs = add([parts[0], near, far, side]).astype(BF)
    return (
        features.transpose(1, 0, 2),
        grad_first,
        grad_second,
        grad_inputs.transpose(1, 0, 2),
    )


def solution(mesh):
    slab = P("chan", "space", None)
    filters = P(None, "chan", None)
    return jax.shard_map(
        shards,
        mesh=mesh,
        in_specs=(slab, filters, filters, slab),
        out_specs=(slab, filters, filters, slab),
        check_vma=False,
    )
```

```python
import functools

import jax
import jax.numpy as jnp
import numpy as np
from jax import lax
from jax.experimental import pallas as pl
from jax.experimental.pallas import tpu as pltpu
from jax.sharding import PartitionSpec as P

SIDE = 32
FLAT = SIDE * SIDE
PLANES = 3
PIECE = 16
SLOTS = 4
BLOCK = SLOTS * PIECE
TAPS = 27
ROWS = 9 * BLOCK
COLS = 3 * BLOCK
NEAR = (0, 1, 2, 3)
FAR = (0, 8, 4, 12)
FIRST, SECOND = (FAR, NEAR), (NEAR, FAR)
LIMIT = 24 * 1024 * 1024
BF = jnp.bfloat16
F32 = jnp.float32


def call(body, outs, scratch, scalars, arrays, flops):
    moved = sum(int(np.prod(x.shape)) * x.dtype.itemsize for x in (*arrays, *outs))
    spec = pl.BlockSpec(memory_space=pltpu.VMEM)
    return pl.pallas_call(
        body,
        out_shape=outs,
        in_specs=[pl.BlockSpec(memory_space=pltpu.SMEM)] * len(scalars) + [spec] * len(arrays),
        out_specs=[spec] * len(outs),
        scratch_shapes=scratch,
        compiler_params=pltpu.CompilerParams(vmem_limit_bytes=LIMIT),
        cost_estimate=pl.CostEstimate(flops=flops, bytes_accessed=moved, transcendentals=0),
    )(*scalars, *arrays)


def shape(dims, dtype=BF):
    return jax.ShapeDtypeStruct(dims, dtype)


def chosen(chan, take, give):
    row = lax.broadcasted_iota(jnp.int32, (256, 256), 0)
    col = lax.broadcasted_iota(jnp.int32, (256, 256), 1)
    n, m = col // BLOCK, (col // PIECE) % SLOTS
    block = chan ^ (n % 2 * give[1]) ^ (n // 2 * give[2]) ^ (m % 2 * take[1]) ^ (m // 2 * take[2])
    return (row == block * PIECE + col % PIECE).astype(BF)


HALF = 14 * PIECE
GRAD_ROWS = 14 * PIECE
HELD = SLOTS * GRAD_ROWS
PLAIN = ((0, 0), (1, 0), (2, 0), (3, 0))
PASSED = ((0, 0), (1, HALF), (1, 0), (2, 0))
ARRIVED = ((0, 0), (2, HALF), (1, 0), (2, 0))
LANES = 2 * BLOCK


def split_body(take, give, spots, chan_ref, weight_ref, *out_refs):
    pick = chosen(chan_ref[0], take, give)
    moved = jnp.dot(weight_ref[...], pick, preferred_element_type=F32).astype(BF)
    for n, (k, row) in enumerate(spots):
        part, out = moved[:, n * BLOCK : (n + 1) * BLOCK], out_refs[k]
        out[row : row + HALF, :BLOCK] = part[:HALF]
        out[row : row + HALF - PIECE, BLOCK:] = part[HALF:]
        out[row + HALF - PIECE : row + HALF, BLOCK:] = jnp.zeros((PIECE, BLOCK), BF)


def split_weight(chan, weight, take, give, sent):
    rows = TAPS * PIECE
    return call(
        functools.partial(split_body, take, give, sent),
        [shape((HALF * sum(k == j for k, _ in sent), LANES)) for j in range(1 + max(sent)[0])],
        [],
        [chan],
        [weight.reshape(rows, 256)],
        2 * rows * 256 * 256,
    )


def stitch_body(left_ref, right_ref, out_ref):
    out_ref[:HALF, :] = left_ref[...]
    out_ref[HALF:, :] = right_ref[HALF:, :]


def stitch(left, right):
    return call(stitch_body, [shape((2 * HALF, LANES))], [], [], [left, right], 0)[0]


def arrange_body(spots, *refs):
    fwd_ref, bwd_ref, held = refs[-3:]
    for a in range(3):
        for b in range(3):
            for c in range(3):
                k = 9 * a + 3 * b + c
                row, lane = PIECE * (k % 14), BLOCK * (k // 14)
                block = jnp.concatenate(
                    [refs[j][at + row : at + row + PIECE, lane : lane + BLOCK] for j, at in spots], axis=0
                )
                at = COLS * b + BLOCK * a
                fwd_ref[BLOCK * c : BLOCK * (c + 1), at : at + BLOCK] = block
                held[BLOCK * k : BLOCK * (k + 1), :] = block
    for a in range(3):
        for b in range(3):

            @pl.loop(0, 3)
            def _(c):
                block = held[pl.ds(pl.multiple_of(BLOCK * (9 * a + 3 * b + c), BLOCK), BLOCK), :]
                at = COLS * (2 - b) + BLOCK * (2 - a)
                rows = pl.ds(pl.multiple_of(BLOCK * (2 - c), BLOCK), BLOCK)
                bwd_ref[rows, at : at + BLOCK] = block.astype(F32).T.astype(BF)


def arrange_weight(pieces, spots):
    return call(
        functools.partial(arrange_body, spots),
        [shape((COLS, ROWS))] * 2,
        [pltpu.VMEM((TAPS * BLOCK, BLOCK), BF)],
        [],
        pieces,
        0,
    )


def edges():
    cell = lax.broadcasted_iota(jnp.int32, (1, FLAT), 1)
    col = cell % SIDE
    return cell, col


def fill(slab, refs, field):
    for p in range(PLANES):
        for m, ref in enumerate(refs[:SLOTS]):
            at = BLOCK * (p + 1) + PIECE * m
            field[at : at + PIECE, :] = ref[p]
    off, core = (ref[...].reshape(BLOCK, FLAT) for ref in refs[SLOTS:])
    off = jnp.where((slab == 0) | (slab == 15), jnp.zeros_like(off), off)
    odd = slab % 2 == 1
    field[:BLOCK, :] = jnp.where(odd, core, off)
    field[BLOCK * (PLANES + 1) :, :] = jnp.where(odd, off, core)


def lift(rows, shift, cell):
    moved = pltpu.roll(rows, -shift % FLAT, 1)
    if shift > 0:
        end = jnp.where(cell[:, -LANES:] < FLAT - SIDE, moved[:, -LANES:], 0.0)
        return jnp.concatenate([moved[:, :-LANES], end], axis=1)
    end = jnp.where(cell[:, :LANES] >= SIDE, moved[:, :LANES], 0.0)
    return jnp.concatenate([end, moved[:, LANES:]], axis=1)


def lift_one(p, up, field, down, cell):
    plane = pl.ds(pl.multiple_of(BLOCK * p, BLOCK), BLOCK)
    rows = field[plane, :].astype(F32)
    down[plane, :] = lift(rows, SIDE, cell).astype(BF)
    up[plane, :] = lift(rows, -SIDE, cell).astype(BF)


def conv_body(space_ref, weight_ref, *refs):
    own_ref, o1, o2, o3, up, field, down = refs[-7:]
    fill(space_ref[0], refs[:-7], field)
    cell, col = edges()
    for p in range(PLANES + 2):
        lift_one(p, up, field, down, cell)
    weight = weight_ref[...]
    for d in range(PLANES):
        window = slice(BLOCK * d, BLOCK * d + COLS)
        terms = sum(
            jnp.dot(weight[:, COLS * b : COLS * (b + 1)], rows[window, :], preferred_element_type=F32)
            for b, rows in enumerate((up, field, down))
        )
        left, mid, right = (terms[BLOCK * c : BLOCK * (c + 1)] for c in range(3))
        left = jnp.where(col >= 1, pltpu.roll(left, 1, 1), 0.0)
        right = jnp.where(col < SIDE - 1, pltpu.roll(right, FLAT - 1, 1), 0.0)
        total = mid + left + right
        own_ref[d] = total[:PIECE]
        for n, out in enumerate((o1, o2, o3), 1):
            out[d] = total[PIECE * n : PIECE * (n + 1)].astype(BF)


def conv(space, weight, slots):
    piece = (PLANES, PIECE, FLAT)
    return call(
        conv_body,
        [shape(piece, F32)] + [shape(piece)] * 3,
        [pltpu.VMEM((BLOCK * (PLANES + 2), FLAT), BF)] * 3,
        [space],
        [weight, *slots],
        2 * ROWS * COLS * FLAT * PLANES,
    )


def across(lhs, rhs):
    return lax.dot_general(lhs, rhs, (((1,), (1,)), ((), ())), preferred_element_type=F32)


def looped(count):
    return pl.loop(0, count)


def straight(count):
    return lambda step: [step(i) for i in range(count)]


def grad_body(spots, each, space_ref, *refs):
    slots, errs = refs[:6], refs[6:10]
    outs, (up, field, down, moved, total) = refs[10:-5], refs[-5:]
    fill(space_ref[0], slots, field)
    cell, col = edges()
    each(PLANES + 2)(lambda p: lift_one(p, up, field, down, cell))
    total[...] = jnp.zeros((COLS, ROWS), F32)

    @each(PLANES)
    def _(d):
        err = jnp.concatenate([e[d] for e in errs], axis=0)
        wide = err.astype(F32)
        left = jnp.where(col < SIDE - 1, pltpu.roll(wide, FLAT - 1, 1), 0.0)
        right = jnp.where(col >= 1, pltpu.roll(wide, 1, 1), 0.0)
        moved[:BLOCK, :] = left.astype(BF)
        moved[BLOCK : 2 * BLOCK, :] = err
        moved[2 * BLOCK :, :] = right.astype(BF)
        window = pl.ds(pl.multiple_of(BLOCK * d, BLOCK), COLS)
        for b, rows in enumerate((up, field, down)):
            part, at = across(moved[...], rows[window, :]), slice(COLS * b, COLS * (b + 1))
            total[:, at] += part
    for n, (k, at) in enumerate(spots):
        part = jnp.concatenate(
            [total[BLOCK * c + PIECE * n : BLOCK * c + PIECE * (n + 1), :] for c in range(3)], axis=0
        ).astype(BF)
        out = outs[k]
        for j in range(4):
            out[at + 48 * j : at + 48 * (j + 1), :] = part[:, LANES * j : LANES * (j + 1)]
        out[at + 192 : at + 224, :BLOCK] = part[:32, 4 * LANES :]
        out[at + 192 : at + 208, BLOCK:] = part[32:, 4 * LANES :]
        out[at + 208 : at + 224, BLOCK:] = jnp.zeros((PIECE, BLOCK), BF)


def weight_grad(space, slots, errs, sent, each):
    return call(
        functools.partial(grad_body, sent, each),
        [shape((HALF * sum(k == j for k, _ in sent), LANES)) for j in range(1 + max(sent)[0])],
        [pltpu.VMEM((BLOCK * (PLANES + 2), FLAT), BF)] * 3
        + [pltpu.VMEM((COLS, FLAT), BF), pltpu.VMEM((COLS, ROWS), F32)],
        [space],
        [*slots, *errs],
        2 * ROWS * COLS * FLAT * PLANES,
    )


def keep_body(space_ref, *refs):
    odd = space_ref[0] % 2 == 1
    pieces, (keep_ref, give_ref) = refs[:-2], refs[-2:]
    for n, (k, at) in enumerate(ARRIVED):

        @pl.loop(0, GRAD_ROWS, step=PIECE * 2)
        def _(i):
            here, there, rows = (
                pl.ds(pl.multiple_of(start + i, PIECE), PIECE * 2) for start in (0, at, n * GRAD_ROWS)
            )
            first, second = pieces[n][here, :], pieces[SLOTS + k][there, :]
            keep_ref[rows, :] = jnp.where(odd, second, first)
            give_ref[rows, :] = jnp.where(odd, first, second)


def total_body(*refs):
    @pl.loop(0, 7)
    def _(i):
        rows = pl.ds(pl.multiple_of(LANES * i, LANES), LANES)
        terms = [ref[rows, :].astype(F32) for ref in refs[:-1]]
        while len(terms) > 1:
            terms = [left + right for left, right in zip(terms[::2], terms[1::2])]
        refs[-1][rows, :] = terms[0].astype(BF)


def total(pieces):
    return call(total_body, [shape((HELD, LANES))], [], [], pieces, 0)[0]


def finish_body(space_ref, chan_ref, mine_ref, got_ref, first_ref, second_ref):
    odd = space_ref[0] % 2 == 1
    first = jnp.where(odd, got_ref[...], mine_ref[...])
    second = jnp.where(odd, mine_ref[...], got_ref[...])
    for held, out, (take, give) in ((first, first_ref, FIRST), (second, second_ref, SECOND)):
        pick = chosen(chan_ref[0], take, give)
        columns = []
        for n in range(SLOTS):
            at = n * GRAD_ROWS
            parts = [
                held[at + 48 * (j // 2) : at + 48 * (j // 2 + 1), BLOCK * (j % 2) : BLOCK * (j % 2 + 1)]
                for j in range(8)
            ]
            parts += [held[at + 192 : at + 224, :BLOCK], held[at + 192 : at + 208, BLOCK:]]
            columns.append(jnp.concatenate(parts, axis=0))
        back = across(jnp.concatenate(columns, axis=1), pick).reshape(TAPS, PIECE, 256)
        for j in range(9):
            k = 9 * (j % 3) + 3 * (j // 3)
            out[k : k + 3] = back[3 * j : 3 * j + 3]


def finish(space, chan, mine, got):
    return call(
        finish_body,
        [shape((TAPS, PIECE, 256), F32)] * 2,
        [],
        [space, chan],
        [mine, got],
        2 * TAPS * PIECE * 256 * 256,
    )


def by_chan(array, mask):
    return lax.ppermute(array, "chan", [(i, i ^ mask) for i in range(16)]) if mask else array


def by_space(array, mask):
    return lax.ppermute(array, "space", [(i, i ^ mask) for i in range(16)])


def over_chan(arrays, masks):
    return [by_chan(array, mask) for array, mask in zip(arrays, masks)]


def gather(array, masks):
    return over_chan([array] * SLOTS, masks)


def edge_body(cross, space_ref, s0, s1, s2, s3, off_ref, core_ref):
    slab = space_ref[0]
    odd, middle = slab % 2 == 1, (slab == 7) | (slab == 8)
    slots = (s0, s1, s2, s3)
    for m, ref in enumerate(slots):
        first, last = ref[0], ref[PLANES - 1]
        outer = jnp.where(odd, last, first)
        if cross:
            peer = slots[m ^ 1]
            outer = jnp.where(middle, jnp.where(odd, peer[PLANES - 1], peer[0]), outer)
        off_ref[m] = outer
        core_ref[m] = jnp.where(odd, first, last)


def outward(slab, chan, cross):
    if slab in (0, 15):
        return 16 * slab + (chan ^ 1)
    there = slab + 1 if slab % 2 else slab - 1
    return 16 * there + (chan ^ (cross and slab in (7, 8)))


def borders(space, slots, cross):
    body = functools.partial(edge_body, cross)
    off, core = call(body, [shape((SLOTS, PIECE, FLAT))] * 2, [], [space], slots, 0)
    pairs = [(16 * i + c, outward(i, c, cross)) for i in range(16) for c in range(16)]
    return [lax.ppermute(off, ("space", "chan"), pairs), by_space(core, 1)]


def add(pieces):
    total = pieces[0].astype(F32)
    for piece in pieces[1:]:
        total = total + piece.astype(F32)
    return total


def slope(value):
    sig = jax.nn.sigmoid(value)
    return sig * (1.0 + value * (1.0 - sig))


tie = lax.optimization_barrier


def shards(inputs, first_weight, second_weight, cotangent):
    space = lax.axis_index("space").astype(jnp.int32).reshape(1)
    chan = lax.axis_index("chan").astype(jnp.int32).reshape(1)
    inputs = inputs.transpose(1, 0, 2)
    cotangent = cotangent.transpose(1, 0, 2)

    in_slots = gather(inputs, FAR)
    pieces = over_chan(split_weight(chan, first_weight, *FIRST, PLAIN), NEAR)
    more = split_weight(chan, second_weight, *SECOND, PASSED)
    in_slots, pieces, more = tie((in_slots, pieces, more))
    in_slots += borders(space, in_slots, False)
    fwd_first, bwd_first = arrange_weight(pieces, PLAIN)
    one = by_chan(more[1], FAR[2])
    in_slots, fwd_first = tie((in_slots, fwd_first))
    sums = over_chan(conv(space, fwd_first, in_slots), NEAR)
    sums[1], one = tie((sums[1], one))
    two = by_chan(stitch(more[2], one), FAR[3])
    pre_first = add(sums)
    hidden = jax.nn.silu(pre_first).astype(BF)

    hid_slots = gather(hidden, NEAR)
    hid_slots, two = tie((hid_slots, two))
    hid_slots += borders(space, hid_slots, True)
    fwd_second, bwd_second = arrange_weight([more[0], one, two], ARRIVED)
    pre_second = add(over_chan(conv(space, fwd_second, hid_slots), FAR))
    features = jax.nn.silu(pre_second).astype(BF)
    err_second = (cotangent.astype(F32) * slope(pre_second)).astype(BF)

    err2_slots = gather(err_second, FAR)
    edge = borders(space, err2_slots, False)
    grads = weight_grad(space, hid_slots, err2_slots, PASSED, looped)
    edge, grads = tie((edge, grads))
    sums = over_chan(conv(space, bwd_second, err2_slots + edge), NEAR)
    one = by_chan(grads[1], FAR[2])
    sums, one = tie((sums, one))
    grad_hidden = add(sums).astype(BF)
    err_first = (grad_hidden.astype(F32) * slope(pre_first)).astype(BF)

    err1_slots = gather(err_first, NEAR)
    two = by_chan(stitch(grads[2], one), FAR[3])
    err1_slots, two = tie((err1_slots, two))
    firsts, err1_slots = tie((weight_grad(space, in_slots, err1_slots, PLAIN, straight), err1_slots))
    firsts = over_chan(firsts, NEAR)
    edge = borders(space, err1_slots, True)
    firsts, edge = tie((firsts, edge))
    keep, give = call(
        keep_body, [shape((HELD, LANES))] * 2, [], [space], [*firsts, grads[0], one, two], 0
    )
    got, parts = tie((by_space(give, 1), conv(space, bwd_first, err1_slots + edge)))
    mine, parts = tie((total([keep, got]), parts))
    got, near = tie((by_space(mine, 8), by_chan(parts[2], FAR[2])))
    mine = total([mine, got])
    mine, parts = tie((mine, parts))
    rest = [by_space(mine, 2 * m) for m in (1, 2, 3)]
    rest, far, side = tie((rest, by_chan(parts[1], FAR[1]), by_chan(parts[3], FAR[3])))
    mine = total([mine, *rest])
    grad_first, grad_second = finish(space, chan, mine, by_space(mine, 1))
    grad_inputs = add([parts[0], near, far, side]).astype(BF)
    return (
        features.transpose(1, 0, 2),
        grad_first,
        grad_second,
        grad_inputs.transpose(1, 0, 2),
    )


def solution(mesh):
    slab = P("chan", "space", None)
    filters = P(None, "chan", None)
    return jax.shard_map(
        shards,
        mesh=mesh,
        in_specs=(slab, filters, filters, slab),
        out_specs=(slab, filters, filters, slab),
        check_vma=False,
    )
```
